256 devices in a mesh: replica: 16 (over x_lo, z), fsdp: 16 (over x_hi, y, core).
Axes of the slice: x: 4 (x_hi: 2, x_lo: 2; x = x_hi * 2 + x_lo), y: 4, z: 8, core: 2. Of those that a mesh axis runs over, the one named last changes fastest.
Arguments:
- token_in: bfloat16 [16, 2048, 8192], P('replica', 'fsdp'), may hold values from -6 to 6
- cotangent: bfloat16 [16, 2048, 512], P('replica', 'fsdp'), may hold values from -6 to 6
- weight: float32 [16, 8192, 512], P('replica', 'fsdp'), may hold values from -4 to 4
- adam_m: float32 [16, 8192, 512], P('replica', 'fsdp'), may hold values from -3 to 3
- adam_v: float32 [16, 8192, 512], P('replica', 'fsdp'), may hold values from 0.05 to 1
- pseudo_grad: float32 [16, 8192, 128], P('replica', 'fsdp'), may hold values from -2 to 2
- momentum: float32 [8192, 128], P('fsdp'), may hold values from -2 to 2
- global_frag: float32 [8192, 128], P('fsdp'), may hold values from -4 to 4
- frag_index: int32 [1], replicated, may hold values from 0 to 3
Outputs:
- values: bfloat16 [16, 2048, 512], P('replica', 'fsdp')
- input_grad: bfloat16 [16, 2048, 8192], P('replica', 'fsdp')
- new_weight: float32 [16, 8192, 512], P('replica', 'fsdp')
- new_m: float32 [16, 8192, 512], P('replica', 'fsdp')
- new_v: float32 [16, 8192, 512], P('replica', 'fsdp')
- new_global: float32 [8192, 128], P('fsdp')
- new_momentum: float32 [8192, 128], P('fsdp')
The draws below stay inside these ranges and needn't reach their ends.
All inputs are finite; a program needn't handle non-finite values.
Results may differ from the reference program's by a relative error of at most 0.006.
Values may be sent and summed in bfloat16 or wider, within the bound.
No kernel may reach another device: no remote copies, remote signals or barrier semaphores. Data moves between devices by JAX's collectives and lax.ppermute only.
A program may use at most 128 MiB of HBM per device.

```python
import math
import jax
import jax.numpy as jnp
from jax import lax

D = 8192
HEAD_DIM = 128
HEADS = 4
F = 512
RTOK = 2048
REPLICAS = 16


def strengthened(drawn, key, source, target, parts, factor):
    def block_of(dim):
        return (jnp.arange(drawn.shape[dim]) // (drawn.shape[dim] // parts)).reshape((-1,) + (1,) * (drawn.ndim - 1 - dim))

    near = jax.random.permutation(key, parts)[block_of(target)]
    far = (block_of(target) + parts // 2) % parts
    return jnp.where((block_of(source) == near) | (block_of(source) == far), factor * drawn, drawn)


def steps_of(rng, extent, cuts, low, high):
    level = 1.0
    for dim, parts in cuts:
        steps = jax.random.uniform(jax.random.fold_in(jax.random.fold_in(rng, 6), dim), (parts,), jnp.float32, low / len(cuts), high / len(cuts))
        level = level * jnp.repeat(jnp.exp(steps), extent[dim] // parts).reshape((-1,) + (1,) * (len(extent) - 1 - dim))
    return level


def gaussian(stream_key, shape, width, most, cuts=(), dtype=jnp.bfloat16):
    level = steps_of(stream_key, shape, cuts, -0.22, 0.18) if cuts else 1.0
    drawn = jax.random.normal(stream_key, shape, jnp.float32) * width * level
    return jnp.minimum(jnp.maximum(drawn, -most), most).astype(dtype)


def heavy_noise(rng, shape, scale, most, pieces, heavy, held_as=jnp.bfloat16):
    result = scale * jax.random.normal(rng, shape, jnp.float32)
    if pieces:
        result = result * steps_of(rng, shape, pieces, -0.22, 0.18)
    return jnp.clip(strengthened(result, jax.random.fold_in(rng, 3), *heavy), -most, most).astype(held_as)


def setup_inputs(seed: int = 0) -> dict:
    seeds = jax.random.split(jax.random.key(seed), 10)
    token_in = heavy_noise(seeds[0], (REPLICAS, RTOK, D), 1.0, 6.0, ((0, 16), (1, 16)), (1, 2, 16, 2.0))
    cotangent = gaussian(seeds[1], (REPLICAS, RTOK, F), 1.0, 6.0, ((0, 16), (1, 16)))
    weight = gaussian(seeds[2], (REPLICAS, D, F), 1.0, 4.0, ((0, 16), (1, 16)), jnp.float32)
    adam_m = gaussian(seeds[3], (REPLICAS, D, F), 0.5, 3.0, ((0, 16), (1, 16)), jnp.float32)
    adam_v = jnp.clip(jnp.exp(math.log(1.0) - 2.9957323 * jax.random.uniform(seeds[4], (REPLICAS, D, F), jnp.float32) ** steps_of(seeds[4], (REPLICAS, D, F), ((0, 16), (1, 16)), -0.2, 0.2)), 0.05, 1.0)
    pseudo_grad = gaussian(seeds[5], (REPLICAS, D, HEAD_DIM), 0.3, 2.0, ((0, 16), (1, 16)), jnp.float32)
    momentum = gaussian(seeds[6], (D, HEAD_DIM), 0.3, 2.0, ((0, 16),), jnp.float32)
    global_frag = gaussian(seeds[7], (D, HEAD_DIM), 1.0, 4.0, ((0, 16),), jnp.float32)
    frag_index = jax.random.randint(seeds[8], (1,), 0, HEADS).astype(jnp.int32)
    return dict(token_in=token_in, cotangent=cotangent, weight=weight, adam_m=adam_m, adam_v=adam_v, pseudo_grad=pseudo_grad, momentum=momentum, global_frag=global_frag, frag_index=frag_index)


beta_first = 0.9
beta_second = 0.95
epsilon = 1e-08
inner_rate = 0.01
decay_rate = 0.1
outer_rate = 0.7
outer_mom = 0.9
mix_share = 0.5

def inner_step(operands):
    tokens, upstream, master, moment_one, moment_two = operands
    scale = D ** (-0.5)
    weight_bf = master.astype(jnp.bfloat16)
    values = (jnp.dot(tokens, weight_bf, preferred_element_type=jnp.float32) * scale).astype(jnp.bfloat16)
    input_grad = (jnp.einsum('tf,rf->tr', upstream, weight_bf, preferred_element_type=jnp.float32) * scale).astype(jnp.bfloat16)
    grad = jnp.einsum('tr,tf->rf', tokens, upstream, preferred_element_type=jnp.float32) * scale
    new_m = beta_first * moment_one + (1.0 - beta_first) * grad
    new_v = beta_second * moment_two + (1.0 - beta_second) * grad * grad
    stepped = master - inner_rate * (new_m / (jnp.sqrt(new_v) + epsilon) + decay_rate * master)
    return (values, input_grad, stepped, new_m, new_v)

def reference(token_in, cotangent, weight, adam_m, adam_v, pseudo_grad, momentum, global_frag, frag_index):
    values, input_grad, stepped, new_m, new_v = lax.map(inner_step, (token_in, cotangent, weight, adam_m, adam_v))
    average = lax.optimization_barrier(jnp.sum(pseudo_grad, axis=0)) / REPLICAS
    new_momentum = outer_mom * momentum + average
    new_global = global_frag - outer_rate * (outer_mom * new_momentum + average)
    start = (frag_index[0] * HEAD_DIM).astype(jnp.int32)
    piece = lax.dynamic_slice_in_dim(stepped, start, HEAD_DIM, 2)
    mixed = mix_share * piece + (1.0 - mix_share) * new_global[None]
    new_weight = lax.dynamic_update_slice_in_dim(stepped, mixed, start, 2)
    return (values, input_grad, new_weight, new_m, new_v, new_global, new_momentum)
```

```python
import jax
import jax.numpy as jnp
from jax import lax
from jax.sharding import PartitionSpec as P

D = 8192

beta_first = 0.9
beta_second = 0.95
epsilon = 1e-08
inner_rate = 0.01
decay_rate = 0.1
outer_rate = 0.7
outer_mom = 0.9
mix_share = 0.5

NY = 4


def fsdp_permute(value, target):
    pairs = []
    for i in range(16):
        x, y, c = i // 8, (i // 2) % NY, i % 2
        x2, y2, c2 = target(x, y, c)
        pairs.append((i, ((x2 % 2) * NY + y2 % NY) * 2 + c2 % 2))
    return lax.ppermute(value, "fsdp", pairs)


def swap_x(value):
    return fsdp_permute(value, lambda x, y, c: (x + 1, y, c))


def swap_core(value):
    return fsdp_permute(value, lambda x, y, c: (x, y, c + 1))


def shift_y(value, step):
    return fsdp_permute(value, lambda x, y, c: (x, y + step, c))


def replica_sum(value):
    total = value
    for bit in (4, 2, 1, 8):
        sent = total.astype(jnp.bfloat16)
        other = lax.ppermute(sent, "replica", [(i, i ^ bit) for i in range(16)])
        total = sent.astype(jnp.float32) + other.astype(jnp.float32)
    return total


def outer_update(momentum, global_frag, average):
    mom_new = outer_mom * momentum + average
    glob_new = global_frag - outer_rate * (outer_mom * mom_new + average)
    return (mom_new, glob_new)


def body(
    token_in, cotangent, weight, adam_m, adam_v, pseudo_grad, momentum, global_frag, frag_index
):
    scale = D ** (-0.5)
    tokens = token_in[0]
    upstream = cotangent[0]
    master = weight[0]
    device = lax.axis_index("fsdp")
    x_hi, y_at, core = device // 8, (device // 2) % NY, device % 2
    half = D // 2

    up_x = swap_x(upstream)
    tok_x = swap_x(lax.dynamic_slice_in_dim(tokens, (1 - x_hi) * half, half, 1))
    tok_o = lax.dynamic_slice_in_dim(tokens, x_hi * half, half, 1)

    weight_bf = master.astype(jnp.bfloat16)
    gathered = jnp.zeros((NY, 512, 512), jnp.bfloat16)
    for step, part in ((0, weight_bf), (1, None), (-1, None), (2, None)):
        part = shift_y(weight_bf, -step) if part is None else part
        gathered = lax.dynamic_update_slice_in_dim(gathered, part[None], (y_at + step) % NY, 0)
    other = swap_core(gathered)
    rows = jnp.zeros((NY, 2, 512, 512), jnp.bfloat16)
    rows = lax.dynamic_update_slice_in_dim(rows, gathered[:, None], core, 1)
    rows = lax.dynamic_update_slice_in_dim(rows, other[:, None], 1 - core, 1)
    rows = rows.reshape(half, 512)

    def back(up):
        return (
            jnp.einsum("tf,rf->tr", up, rows, preferred_element_type=jnp.float32) * scale
        ).astype(jnp.bfloat16)

    back_x = swap_x(back(up_x))
    block = jnp.zeros((128, D), jnp.bfloat16)
    block = lax.dynamic_update_slice_in_dim(block, back(upstream), x_hi * half, 1)
    block = lax.dynamic_update_slice_in_dim(block, back_x, (1 - x_hi) * half, 1)

    part_x = jnp.dot(tok_x, rows, preferred_element_type=jnp.float32).astype(jnp.bfloat16)
    part_o = jnp.dot(tok_o, rows, preferred_element_type=jnp.float32)
    values = ((part_o + swap_x(part_x).astype(jnp.float32)) * scale).astype(jnp.bfloat16)

    tok_2 = jnp.stack([tok_o, tok_x]).reshape(2, 128, NY, 2, 512)
    up_2 = jnp.stack([upstream, up_x])
    tok_mine = lax.dynamic_index_in_dim(tok_2, core, 3, False)
    tok_other = swap_core(lax.dynamic_index_in_dim(tok_2, 1 - core, 3, False))
    up_other = swap_core(up_2)
    tok_4 = jnp.concatenate([tok_mine, tok_other]).reshape(512, NY, 512)
    up_4 = jnp.concatenate([up_2, up_other]).reshape(512, 512)

    def grad_of(step):
        cols = lax.dynamic_index_in_dim(tok_4, (y_at + step) % NY, 1, False)
        return jnp.einsum("tr,tf->rf", cols, up_4, preferred_element_type=jnp.float32) * scale

    grad = grad_of(0)
    for step in (2, 1, -1):
        grad = grad + shift_y(grad_of(step).astype(jnp.bfloat16), step).astype(jnp.float32)

    total = replica_sum(pseudo_grad[0])
    new_momentum, new_global = outer_update(momentum, global_frag, total / 16)

    new_m = beta_first * adam_m[0] + (1.0 - beta_first) * grad
    new_v = beta_second * adam_v[0] + (1.0 - beta_second) * grad * grad
    stepped = master - inner_rate * (new_m / (jnp.sqrt(new_v) + epsilon) + decay_rate * master)
    frag_width = global_frag.shape[1]
    start = frag_index[0] * frag_width
    piece = lax.dynamic_slice_in_dim(stepped, start, frag_width, 1)
    mixed = mix_share * piece + (1.0 - mix_share) * new_global
    new_weight = lax.dynamic_update_slice_in_dim(stepped, mixed, start, 1)
    return (
        values[None],
        block[None],
        new_weight[None],
        new_m[None],
        new_v[None],
        new_global,
        new_momentum,
    )


def solution(mesh):
    in_specs = (
        P("replica", "fsdp", None),
        P("replica", "fsdp", None),
        P("replica", "fsdp", None),
        P("replica", "fsdp", None),
        P("replica", "fsdp", None),
        P("replica", "fsdp", None),
        P("fsdp", None),
        P("fsdp", None),
        P(),
    )
    out_specs = (
        P("replica", "fsdp", None),
        P("replica", "fsdp", None),
        P("replica", "fsdp", None),
        P("replica", "fsdp", None),
        P("replica", "fsdp", None),
        P("fsdp", None),
        P("fsdp", None),
    )
    return jax.shard_map(body, mesh=mesh, in_specs=in_specs, out_specs=out_specs, check_vma=False)
```

```python
import functools

import jax
import jax.numpy as jnp
from jax import lax
from jax.experimental import pallas as pl
from jax.experimental.pallas import tpu as pltpu
from jax.sharding import PartitionSpec as P

D = 8192
SCALE = D ** (-0.5)

beta_first = 0.9
beta_second = 0.95
epsilon = 1e-08
inner_rate = 0.01
decay_rate = 0.1
outer_rate = 0.7
outer_mom = 0.9
mix_share = 0.5

NY = 4
TOK = 128
ROWS = 512
F = 512
PIECE = NY * ROWS
VMEM = pltpu.CompilerParams(vmem_limit_bytes=40 * 1024 * 1024)


def fsdp_permute(value, target):
    pairs = []
    for i in range(16):
        x, y, c = i // 8, (i // 2) % NY, i % 2
        x2, y2, c2 = target(x, y, c)
        pairs.append((i, ((x2 % 2) * NY + y2 % NY) * 2 + c2 % 2))
    return lax.ppermute(value, "fsdp", pairs)


def swap_x(value):
    return fsdp_permute(value, lambda x, y, c: (x + 1, y, c))


def swap_core(value):
    return fsdp_permute(value, lambda x, y, c: (x, y, c + 1))


def shift_y(value, step):
    return fsdp_permute(value, lambda x, y, c: (x, y + step, c))


def replica_step(total, bit):
    sent = total.astype(jnp.bfloat16)
    other = lax.ppermute(sent, "replica", [(i, i ^ bit) for i in range(16)])
    return sent.astype(jnp.float32) + other.astype(jnp.float32)


def after(value, *others):
    return lax.optimization_barrier((value, *others))[0]


def outer_update(momentum, global_frag, average):
    mom_new = outer_mom * momentum + average
    glob_new = global_frag - outer_rate * (outer_mom * mom_new + average)
    return (mom_new, glob_new)


def shape(rows, cols, dtype=jnp.bfloat16):
    return jax.ShapeDtypeStruct((rows, cols), dtype)


SMALL = pl.CostEstimate(flops=1, bytes_accessed=1, transcendentals=0)


def here():
    device = lax.axis_index("fsdp")
    return device // (2 * NY), lax.rem(device // 2, NY), lax.rem(device, 2)


def column(x, y, c):
    return pl.ds(pl.multiple_of(((x * NY + y) * 2 + c) * ROWS, ROWS), ROWS)


def pieces_of(tokens, wanted):
    def kernel(source, *refs):
        targets, sems = refs[:-1], refs[-1]
        x, _, c = here()
        copies = []
        for i, ((dx, dc), target) in enumerate(zip(wanted, targets, strict=True)):
            for k in range(NY):
                copies.append(
                    pltpu.make_async_copy(
                        source.at[:, column(1 - x if dx else x, k, 1 - c if dc else c)],
                        target.at[:, pl.ds(k * ROWS, ROWS)],
                        sems.at[i * NY + k],
                    )
                )
        for copy in copies:
            copy.start()
        for copy in copies:
            copy.wait()

    return pl.pallas_call(
        kernel,
        in_specs=[pl.BlockSpec(memory_space=pltpu.HBM)],
        out_specs=[pl.BlockSpec(memory_space=pltpu.VMEM)] * len(wanted),
        out_shape=[shape(TOK, PIECE) for _ in wanted],
        scratch_shapes=[pltpu.SemaphoreType.DMA((NY * len(wanted),))],
        cost_estimate=SMALL,
        compiler_params=VMEM,
        name="pieces",
    )(tokens)


def input_grad_pieces(up, blocks):
    def kernel(up_ref, w0, w1, w2, w3, *outs):
        up = up_ref[...]
        for step, w in enumerate((w0, w1, w2, w3)):
            at = pl.multiple_of(lax.rem(here()[1] + step, NY) * ROWS, ROWS)
            grad = lax.dot_general(
                up, w[...], (((1,), (1,)), ((), ())), preferred_element_type=jnp.float32
            )
            grad = (grad * SCALE).astype(jnp.bfloat16)
            for k, out in enumerate(outs):
                out[:, pl.ds(at, ROWS)] = grad[k * TOK : (k + 1) * TOK]

    return pl.pallas_call(
        kernel,
        in_specs=[pl.BlockSpec(memory_space=pltpu.VMEM)] * 5,
        out_specs=[pl.BlockSpec(memory_space=pltpu.VMEM)] * 4,
        out_shape=[shape(TOK, PIECE)] * 4,
        cost_estimate=SMALL,
        compiler_params=VMEM,
        name="input_grad",
    )(up, *blocks)


def weight_grad_blocks(toks, up):
    def kernel(t0, t1, t2, t3, up_ref, g0, g1, g2, g3):
        up = up_ref[...]
        for step, out in ((2, g2), (1, g1), (3, g3), (0, g0)):
            at = pl.multiple_of(lax.rem(here()[1] + step, NY) * ROWS, ROWS)
            tok = jnp.concatenate([t[:, pl.ds(at, ROWS)] for t in (t0, t1, t2, t3)], axis=0)
            grad = lax.dot_general(
                tok, up, (((0,), (0,)), ((), ())), preferred_element_type=jnp.float32
            )
            out[...] = (grad * SCALE).astype(out.dtype)

    return pl.pallas_call(
        kernel,
        in_specs=[pl.BlockSpec(memory_space=pltpu.VMEM)] * 5,
        out_specs=[pl.BlockSpec(memory_space=pltpu.VMEM)] * 4,
        out_shape=[shape(ROWS, F, jnp.float32)] + [shape(ROWS, F)] * 3,
        cost_estimate=SMALL,
        compiler_params=VMEM,
        name="weight_grad",
    )(*toks, up)


def value_parts(toks, blocks):
    def kernel(t0, t1, t2, t3, w0, w1, w2, w3, own, far, core):
        total = jnp.zeros((4 * TOK, F), jnp.float32)
        for step, w in enumerate((w0, w1, w2, w3)):
            at = pl.multiple_of(lax.rem(here()[1] + step, NY) * ROWS, ROWS)
            tok = jnp.concatenate([t[:, pl.ds(at, ROWS)] for t in (t0, t1, t2, t3)], axis=0)
            total += jnp.dot(tok, w[...], preferred_element_type=jnp.float32)
        own[...] = total[:TOK]
        far[...] = total[TOK : 2 * TOK]
        core[...] = total[2 * TOK :]

    return pl.pallas_call(
        kernel,
        in_specs=[pl.BlockSpec(memory_space=pltpu.VMEM)] * 8,
        out_specs=[pl.BlockSpec(memory_space=pltpu.VMEM)] * 3,
        out_shape=[shape(TOK, F, jnp.float32)] * 2 + [shape(2 * TOK, F, jnp.float32)],
        cost_estimate=SMALL,
        compiler_params=VMEM,
        name="values",
    )(*toks, *blocks)


def assemble(block, parts, wanted):
    def kernel(*refs):
        sources, target, sems = refs[: len(wanted)], refs[-2], refs[-1]
        x, _, c = here()
        copies = []
        for i, ((dx, dc), source) in enumerate(zip(wanted, sources, strict=True)):
            for k in range(NY):
                copies.append(
                    pltpu.make_async_copy(
                        source.at[:, pl.ds(k * ROWS, ROWS)],
                        target.at[:, column(1 - x if dx else x, k, 1 - c if dc else c)],
                        sems.at[i * NY + k],
                    )
                )
        for copy in copies:
            copy.start()
        for copy in copies:
            copy.wait()

    ins = [pl.BlockSpec(memory_space=pltpu.VMEM)] * len(wanted)
    args, alias = list(parts), {}
    if block is not None:
        ins.append(pl.BlockSpec(memory_space=pltpu.HBM))
        args.append(block)
        alias = {len(wanted): 0}
    return pl.pallas_call(
        kernel,
        in_specs=ins,
        out_specs=pl.BlockSpec(memory_space=pltpu.HBM),
        out_shape=shape(TOK, D),
        scratch_shapes=[pltpu.SemaphoreType.DMA((NY * len(wanted),))],
        input_output_aliases=alias,
        cost_estimate=SMALL,
        compiler_params=VMEM,
        name="assemble",
    )(*args)


STRIP = 64


def adam(frag_index, grads, adam_m, adam_v, master, new_global):
    def kernel(frag, g0, g1, g2, g3, m, v, w, glob, hbm_w, hbm_m, hbm_v, new_w, new_m, new_v, sems):
        at = pl.ds(pl.multiple_of(frag[0] * 128, 128), 128)
        copies = []
        for k in range(ROWS // STRIP):
            rows = pl.ds(k * STRIP, STRIP)
            grad = g0[rows, :] + g1[rows, :].astype(jnp.float32)
            grad = grad + g2[rows, :].astype(jnp.float32)
            grad = grad + g3[rows, :].astype(jnp.float32)
            mom = beta_first * m[rows, :] + (1.0 - beta_first) * grad
            var = beta_second * v[rows, :] + (1.0 - beta_second) * grad * grad
            new_m[rows, :] = mom
            new_v[rows, :] = var
            old = w[rows, :]
            new_w[rows, :] = old - inner_rate * (
                mom / (jnp.sqrt(var) + epsilon) + decay_rate * old
            )
            new_w[rows, at] = mix_share * new_w[rows, at] + (1.0 - mix_share) * glob[rows, :]
            for i, (source, target) in enumerate(
                ((new_w, hbm_w), (new_m, hbm_m), (new_v, hbm_v))
            ):
                copy = pltpu.make_async_copy(source.at[rows], target.at[rows], sems.at[i, k])
                copy.start()
                copies.append(copy)
        for copy in copies:
            copy.wait()

    return pl.pallas_call(
        kernel,
        in_specs=[pl.BlockSpec(memory_space=pltpu.SMEM)]
        + [pl.BlockSpec(memory_space=pltpu.VMEM)] * 8,
        out_specs=[pl.BlockSpec(memory_space=pltpu.HBM)] * 3,
        out_shape=[shape(ROWS, F, jnp.float32)] * 3,
        scratch_shapes=[pltpu.VMEM((ROWS, F), jnp.float32)] * 3
        + [pltpu.SemaphoreType.DMA((3, ROWS // STRIP))],
        cost_estimate=SMALL,
        compiler_params=VMEM,
        name="adam",
    )(frag_index, *grads, adam_m, adam_v, master, new_global)


def body(
    token_in, cotangent, weight, adam_m, adam_v, pseudo_grad, momentum, global_frag, frag_index
):
    tokens = token_in[0]
    up_own = cotangent[0]
    master = weight[0]

    (send_far,) = pieces_of(tokens, ((1, 1),))
    far = swap_x(send_far)
    up_x = swap_x(up_own)
    weight_bf = master.astype(jnp.bfloat16)
    block_1 = shift_y(weight_bf, -1)
    block_3 = shift_y(weight_bf, 1)
    total = replica_step(pseudo_grad[0], 8)
    tok_own, send_core, send_x = pieces_of(after(tokens, send_far), ((0, 0), (0, 1), (1, 0)))
    up_2 = jnp.concatenate([up_own, up_x])
    up_4 = jnp.concatenate([up_2, swap_core(after(up_2, total))])
    tok_core = swap_core(after(send_core, up_4))
    tok_x = swap_x(after(send_x, total))
    total = replica_step(total, 1)
    tok_far = swap_core(far)
    block_2 = shift_y(after(weight_bf, block_1, block_3), 2)
    total = replica_step(total, 2)
    total = replica_step(total, 4)
    new_momentum, new_global = outer_update(momentum, global_frag, total / 16)
    toks = (tok_own, tok_x, tok_core, tok_far)
    blocks = (weight_bf, block_1, block_2, block_3)

    ig_own, ig_x, ig_core, ig_far = input_grad_pieces(up_4, blocks)
    back_far = swap_core(ig_far)
    back_x = swap_x(ig_x)
    back_core = swap_core(ig_core)
    back_other = swap_x(back_far)

    g0, g1, g2, g3 = weight_grad_blocks(toks, after(up_4, new_global))
    r2 = shift_y(g2, 2)
    r1 = shift_y(after(g1, r2), 1)
    r3 = shift_y(after(g3, r2), -1)

    val_own, val_x, val_core = value_parts(toks, blocks)
    val_back = swap_core(val_core)
    val_far = swap_x((val_x + val_back[TOK:]).astype(jnp.bfloat16))
    values = val_own + val_back[:TOK] + val_far.astype(jnp.float32)
    values = (values * SCALE).astype(jnp.bfloat16)

    block = assemble(None, (ig_own, back_core), ((0, 0), (0, 1)))
    new_weight, new_m, new_v = adam(
        frag_index, (g0, r1, r2, r3), adam_m[0], adam_v[0], master, new_global
    )
    block = assemble(block, (back_x, back_other), ((1, 0), (1, 1)))
    return (
        values[None],
        block[None],
        new_weight[None],
        new_m[None],
        new_v[None],
        new_global,
        new_momentum,
    )


def solution(mesh):
    in_specs = (
        P("replica", "fsdp", None),
        P("replica", "fsdp", None),
        P("replica", "fsdp", None),
        P("replica", "fsdp", None),
        P("replica", "fsdp", None),
        P("replica", "fsdp", None),
        P("fsdp", None),
        P("fsdp", None),
        P(),
    )
    out_specs = (
        P("replica", "fsdp", None),
        P("replica", "fsdp", None),
        P("replica", "fsdp", None),
        P("replica", "fsdp", None),
        P("replica", "fsdp", None),
        P("fsdp", None),
        P("fsdp", None),
    )
    return jax.shard_map(body, mesh=mesh, in_specs=in_specs, out_specs=out_specs, check_vma=False)
```

```python
import functools

import jax
import jax.numpy as jnp
from jax import lax
from jax.experimental import pallas as pl
from jax.experimental.pallas import tpu as pltpu
from jax.sharding import PartitionSpec as P

D = 8192
SCALE = D ** (-0.5)

beta_first = 0.9
beta_second = 0.95
epsilon = 1e-08
inner_rate = 0.01
decay_rate = 0.1
outer_rate = 0.7
outer_mom = 0.9
mix_share = 0.5

NY = 4
TOK = 128
ROWS = 512
F = 512
PIECE = NY * ROWS
HALF = ROWS // 2
VMEM = pltpu.CompilerParams(vmem_limit_bytes=40 * 1024 * 1024)


def fsdp_permute(value, target):
    pairs = []
    for i in range(16):
        x, y, c = i // 8, (i // 2) % NY, i % 2
        x2, y2, c2 = target(x, y, c)
        pairs.append((i, ((x2 % 2) * NY + y2 % NY) * 2 + c2 % 2))
    return lax.ppermute(value, "fsdp", pairs)


def swap_x(value):
    return fsdp_permute(value, lambda x, y, c: (x + 1, y, c))


def swap_core(value):
    return fsdp_permute(value, lambda x, y, c: (x, y, c + 1))


def shift_y(value, step):
    return fsdp_permute(value, lambda x, y, c: (x, y + step, c))


def replica_step(total, partner):
    sent = total.astype(jnp.bfloat16)
    other = lax.ppermute(sent, "replica", [(i, partner(i)) for i in range(16)])
    return sent.astype(jnp.float32) + other.astype(jnp.float32)


def after(value, *others):
    return lax.optimization_barrier((value, *others))[0]


def outer_update(momentum, global_frag, average):
    mom_new = outer_mom * momentum + average
    glob_new = global_frag - outer_rate * (outer_mom * mom_new + average)
    return (mom_new, glob_new)


def shape(rows, cols, dtype=jnp.bfloat16):
    return jax.ShapeDtypeStruct((rows, cols), dtype)


SMALL = pl.CostEstimate(flops=1, bytes_accessed=1, transcendentals=0)


def here():
    device = lax.axis_index("fsdp")
    return device // (2 * NY), lax.rem(device // 2, NY), lax.rem(device, 2)


def column(x, y, c):
    return pl.ds(pl.multiple_of(((x * NY + y) * 2 + c) * ROWS, ROWS), ROWS)


def pieces_of(tokens, up, wanted):
    groups = [(i, g) for i, stack in enumerate(wanted) for g in stack]

    def kernel(source, up_ref, *refs):
        targets, sems = refs[:-1], refs[-1]
        x, _, c = here()
        copies, filled = [], [0] * len(wanted)
        for n, (i, (dx, dc, start, size, with_up)) in enumerate(groups):
            rows, into = pl.ds(start, size), pl.ds(filled[i], size)
            filled[i] += size
            moves = [
                (
                    source.at[rows, column(1 - x if dx else x, k, 1 - c if dc else c)],
                    targets[i].at[into, pl.ds(k * ROWS, ROWS)],
                )
                for k in range(NY)
            ]
            if with_up:
                moves.append((up_ref.at[rows], targets[i].at[into, pl.ds(PIECE, F)]))
            for k, (here_from, here_to) in enumerate(moves):
                copies.append(pltpu.make_async_copy(here_from, here_to, sems.at[n, k]))
        for copy in copies:
            copy.start()
        for copy in copies:
            copy.wait()

    return pl.pallas_call(
        kernel,
        in_specs=[pl.BlockSpec(memory_space=pltpu.VMEM), pl.BlockSpec(memory_space=pltpu.HBM)],
        out_specs=[pl.BlockSpec(memory_space=pltpu.VMEM)] * len(wanted),
        out_shape=[
            shape(sum(g[3] for g in stack), PIECE + F * stack[0][4]) for stack in wanted
        ],
        scratch_shapes=[pltpu.SemaphoreType.DMA((len(groups), NY + 1))],
        cost_estimate=SMALL,
        compiler_params=VMEM,
        name="pieces",
    )(tokens, up)


def places(blocks):
    y = here()[1]
    for (step, start), block in zip(((0, 0), (1, 0), (3, 0), (2, 0), (2, HALF)), blocks, strict=True):
        at = pl.multiple_of(lax.rem(y + step, NY) * ROWS + start, HALF)
        yield pl.ds(at, block.shape[0]), block


def input_grad(ups, blocks):
    def kernel(u0, u1, u2, *refs):
        own, far_x, core, far = refs[5:]
        up = jnp.concatenate([u0[...], u1[:, PIECE:], u2[...]], axis=0)
        for at, block in places(refs[:5]):
            grad = lax.dot_general(
                up, block[...], (((1,), (1,)), ((), ())), preferred_element_type=jnp.float32
            )
            grad = (grad * SCALE).astype(jnp.bfloat16)
            own[:, at] = grad[:TOK]
            far_x[:, at] = grad[TOK : 2 * TOK]
            core[:, at] = grad[2 * TOK : 3 * TOK]
            far[:, at] = grad[3 * TOK :]

    return pl.pallas_call(
        kernel,
        in_specs=[pl.BlockSpec(memory_space=pltpu.VMEM)] * 8,
        out_specs=[pl.BlockSpec(memory_space=pltpu.VMEM)] * 4,
        out_shape=[shape(TOK, PIECE)] * 4,
        cost_estimate=SMALL,
        compiler_params=VMEM,
        name="input_grad",
    )(*ups, *blocks)


def value_parts(toks, blocks):
    def kernel(t0, t1, t2, t3, *refs):
        own, far, pair = refs[5:]
        total = jnp.zeros((4 * TOK, F), jnp.float32)
        for at, block in places(refs[:5]):
            tok = jnp.concatenate([t0[:, at], t1[:, at], t2[:, at], t3[:, at]], axis=0)
            total += jnp.dot(tok, block[...], preferred_element_type=jnp.float32)
        own[...] = total[:TOK]
        far[...] = total[TOK : 2 * TOK]
        pair[...] = total[2 * TOK :]

    return pl.pallas_call(
        kernel,
        in_specs=[pl.BlockSpec(memory_space=pltpu.VMEM)] * 9,
        out_specs=[pl.BlockSpec(memory_space=pltpu.VMEM)] * 3,
        out_shape=[shape(TOK, F, jnp.float32)] * 2 + [shape(2 * TOK, F, jnp.float32)],
        cost_estimate=SMALL,
        compiler_params=VMEM,
        name="values",
    )(*toks, *blocks)


def weight_grad_blocks(toks, ups):
    def kernel(t0, t1, t2, t3, u0, u2, g0, g1, g3, up_half, down_half):
        up = jnp.concatenate([u0[...], t1[:, PIECE:], u2[...]], axis=0)
        y = here()[1]
        for step in (2, 1, 3, 0):
            at = pl.ds(pl.multiple_of(lax.rem(y + step, NY) * ROWS, ROWS), ROWS)
            tok = jnp.concatenate([t0[:, at], t1[:, at], t2[:, at], t3[:, at]], axis=0)
            grad = SCALE * lax.dot_general(
                tok, up, (((0,), (0,)), ((), ())), preferred_element_type=jnp.float32
            )
            if step == 2:
                up_half[...] = grad[:HALF].astype(jnp.bfloat16)
                down_half[...] = grad[HALF:].astype(jnp.bfloat16)
            else:
                {0: g0, 1: g1, 3: g3}[step][...] = grad

    return pl.pallas_call(
        kernel,
        in_specs=[pl.BlockSpec(memory_space=pltpu.VMEM)] * 6,
        out_specs=[pl.BlockSpec(memory_space=pltpu.VMEM)] * 5,
        out_shape=[shape(ROWS, F, jnp.float32)] * 3 + [shape(HALF, F)] * 2,
        cost_estimate=SMALL,
        compiler_params=VMEM,
        name="weight_grad",
    )(*toks, *ups)


def relay(g1, g3, from_below, from_above):
    def kernel(g1, g3, from_below, from_above, s1, s3):
        s1[:HALF] = (g1[:HALF] + from_below[...].astype(jnp.float32)).astype(jnp.bfloat16)
        s1[HALF:] = g1[HALF:].astype(jnp.bfloat16)
        s3[:HALF] = g3[:HALF].astype(jnp.bfloat16)
        s3[HALF:] = (g3[HALF:] + from_above[...].astype(jnp.float32)).astype(jnp.bfloat16)

    return pl.pallas_call(
        kernel,
        in_specs=[pl.BlockSpec(memory_space=pltpu.VMEM)] * 4,
        out_specs=[pl.BlockSpec(memory_space=pltpu.VMEM)] * 2,
        out_shape=[shape(ROWS, F)] * 2,
        cost_estimate=SMALL,
        compiler_params=VMEM,
        name="relay",
    )(g1, g3, from_below, from_above)


def assemble(block, parts, wanted):
    n = len(wanted)
    groups = [(i, j, g) for i, stack in enumerate(wanted) for j, g in enumerate(stack)]

    def kernel(*refs):
        target, sems = refs[-2:]
        x, _, c = here()
        copies = []
        for m, (i, j, (dx, dc)) in enumerate(groups):
            for k in range(NY):
                copies.append(
                    pltpu.make_async_copy(
                        refs[i].at[pl.ds(j * TOK, TOK), pl.ds(k * ROWS, ROWS)],
                        target.at[:, column(1 - x if dx else x, k, 1 - c if dc else c)],
                        sems.at[m * NY + k],
                    )
                )
        for copy in copies:
            copy.start()
        for copy in copies:
            copy.wait()

    args = list(parts)
    ins = [pl.BlockSpec(memory_space=pltpu.VMEM)] * n
    alias = {}
    if block is not None:
        alias = {n: 0}
        ins.append(pl.BlockSpec(memory_space=pltpu.HBM))
        args.append(block)
    return pl.pallas_call(
        kernel,
        in_specs=ins,
        out_specs=pl.BlockSpec(memory_space=pltpu.HBM),
        out_shape=shape(TOK, D),
        scratch_shapes=[pltpu.SemaphoreType.DMA((NY * len(groups),))],
        input_output_aliases=alias,
        cost_estimate=SMALL,
        compiler_params=VMEM,
        name="assemble",
    )(*args)


STRIP = 64


def adam(frag_index, grads, adam_m, adam_v, master, new_global):
    def kernel(frag, g0, g1, g3, m, v, w, glob, hbm_w, hbm_m, hbm_v, new_w, new_m, new_v, sems):
        at = pl.ds(pl.multiple_of(frag[0] * 128, 128), 128)
        copies = []
        for k in range(ROWS // STRIP):
            rows = pl.ds(k * STRIP, STRIP)
            grad = g0[rows, :] + g1[rows, :].astype(jnp.float32)
            grad = grad + g3[rows, :].astype(jnp.float32)
            mom = beta_first * m[rows, :] + (1.0 - beta_first) * grad
            var = beta_second * v[rows, :] + (1.0 - beta_second) * grad * grad
            new_m[rows, :] = mom
            new_v[rows, :] = var
            old = w[rows, :]
            new_w[rows, :] = old - inner_rate * (
                mom / (jnp.sqrt(var) + epsilon) + decay_rate * old
            )
            new_w[rows, at] = mix_share * new_w[rows, at] + (1.0 - mix_share) * glob[rows, :]
            for i, (source, target) in enumerate(
                ((new_w, hbm_w), (new_m, hbm_m), (new_v, hbm_v))
            ):
                copy = pltpu.make_async_copy(source.at[rows], target.at[rows], sems.at[i, k])
                copy.start()
                copies.append(copy)
        for copy in copies:
            copy.wait()

    return pl.pallas_call(
        kernel,
        in_specs=[pl.BlockSpec(memory_space=pltpu.SMEM)]
        + [pl.BlockSpec(memory_space=pltpu.VMEM)] * 7,
        out_specs=[pl.BlockSpec(memory_space=pltpu.HBM)] * 3,
        out_shape=[shape(ROWS, F, jnp.float32)] * 3,
        scratch_shapes=[pltpu.VMEM((ROWS, F), jnp.float32)] * 3
        + [pltpu.SemaphoreType.DMA((3, ROWS // STRIP))],
        cost_estimate=SMALL,
        compiler_params=VMEM,
        name="adam",
    )(frag_index, *grads, adam_m, adam_v, master, new_global)


def body(
    token_in, cotangent, weight, adam_m, adam_v, pseudo_grad, momentum, global_frag, frag_index
):
    tokens = token_in[0]
    up_own = cotangent[0]
    master = weight[0]

    send_x, send_far = pieces_of(tokens, up_own, [((1, 0, 0, TOK, 1),), ((1, 1, 0, TOK, 0),)])
    tok_x = swap_x(send_x)
    for_core = swap_x(send_far)
    weight_bf = after(master.astype(jnp.bfloat16), send_x)
    block_1 = shift_y(weight_bf, -1)
    block_3 = shift_y(weight_bf, 1)
    tok_own, send_core = pieces_of(
        after(tokens, send_x), up_own, [((0, 0, 0, TOK, 0),), ((0, 1, 0, TOK, 0),)]
    )
    tok_core = swap_core(send_core)
    up_pair = swap_core(jnp.concatenate([up_own, tok_x[:, PIECE:]]))
    block_2a = shift_y(block_1[:HALF], -1)
    block_2b = shift_y(block_3[HALF:], 1)
    blocks = (weight_bf, block_1, block_3, block_2a, block_2b)

    total = replica_step(after(pseudo_grad[0].astype(jnp.bfloat16), tok_core), lambda i: i ^ 6)
    up_ready, total = lax.optimization_barrier((up_own, total))

    ig_own, ig_x, ig_core, ig_far = input_grad((up_ready, tok_x, up_pair), blocks)
    back_x = swap_x(ig_x)
    back_far = swap_core(ig_far)
    back_other = swap_x(back_far)
    back_core = swap_core(ig_core)

    tok_far = swap_core(after(for_core, ig_own))
    toks = (tok_own, tok_x, tok_core, tok_far)
    g0, g1, g3, up_half, down_half = weight_grad_blocks(toks, (after(up_own, back_far), up_pair))
    s1, s3 = relay(after(g1, back_x), g3, shift_y(up_half, 1), shift_y(down_half, -1))
    r1 = shift_y(s1, 1)
    r3 = shift_y(s3, -1)

    total = replica_step(after(total, back_far), lambda i: i ^ 1)
    block_0 = after(weight_bf, g0, back_core)
    val_own, val_x, val_pair = value_parts(toks, (block_0, *blocks[1:]))
    val_back = swap_core(val_pair)
    total = replica_step(after(total, val_back), lambda i: i ^ 2)
    total = replica_step(after(total, s1), lambda i: i ^ 8)
    new_momentum, new_global = outer_update(momentum, global_frag, total / 16)

    val_far = swap_x((val_x + val_back[TOK:]).astype(jnp.bfloat16))
    values = val_own + val_back[:TOK] + val_far.astype(jnp.float32)
    values = (values * SCALE).astype(jnp.bfloat16)

    block = assemble(None, (ig_own, back_core, back_x), [((0, 0),), ((0, 1),), ((1, 0),)])
    new_weight, new_m, new_v = adam(
        frag_index, (g0, r1, r3), adam_m[0], adam_v[0], master, new_global
    )
    block = assemble(block, (after(back_other, new_weight),), [((1, 1),)])
    return (
        values[None],
        block[None],
        new_weight[None],
        new_m[None],
        new_v[None],
        new_global,
        new_momentum,
    )


def solution(mesh):
    in_specs = (
        P("replica", "fsdp", None),
        P("replica", "fsdp", None),
        P("replica", "fsdp", None),
        P("replica", "fsdp", None),
        P("replica", "fsdp", None),
        P("replica", "fsdp", None),
        P("fsdp", None),
        P("fsdp", None),
        P(),
    )
    out_specs = (
        P("replica", "fsdp", None),
        P("replica", "fsdp", None),
        P("replica", "fsdp", None),
        P("replica", "fsdp", None),
        P("replica", "fsdp", None),
        P("fsdp", None),
        P("fsdp", None),
    )
    return jax.shard_map(body, mesh=mesh, in_specs=in_specs, out_specs=out_specs, check_vma=False)
```

```python
import functools

import jax
import jax.numpy as jnp
from jax import lax
from jax.experimental import pallas as pl
from jax.experimental.pallas import tpu as pltpu
from jax.sharding import PartitionSpec as P

D = 8192
SCALE = D ** (-0.5)

beta_first = 0.9
beta_second = 0.95
epsilon = 1e-08
inner_rate = 0.01
decay_rate = 0.1
outer_rate = 0.7
outer_mom = 0.9
mix_share = 0.5

NY = 4
TOK = 128
ROWS = 512
F = 512
PIECE = NY * ROWS
HALF = ROWS // 2
FIRST = 96
LATER = 320
VMEM = pltpu.CompilerParams(vmem_limit_bytes=40 * 1024 * 1024)


def fsdp_permute(value, target):
    pairs = []
    for i in range(16):
        x, y, c = i // 8, (i // 2) % NY, i % 2
        x2, y2, c2 = target(x, y, c)
        pairs.append((i, ((x2 % 2) * NY + y2 % NY) * 2 + c2 % 2))
    return lax.ppermute(value, "fsdp", pairs)


def swap_x(value):
    return fsdp_permute(value, lambda x, y, c: (x + 1, y, c))


def swap_core(value):
    return fsdp_permute(value, lambda x, y, c: (x, y, c + 1))


def shift_y(value, step):
    return fsdp_permute(value, lambda x, y, c: (x, y + step, c))


def replica_step(total, partner):
    sent = total.astype(jnp.bfloat16)
    other = lax.ppermute(sent, "replica", [(i, partner(i)) for i in range(16)])
    return sent.astype(jnp.float32) + other.astype(jnp.float32)


def after(value, *others):
    return lax.optimization_barrier((value, *others))[0]


def outer_update(momentum, global_frag, average):
    mom_new = outer_mom * momentum + average
    glob_new = global_frag - outer_rate * (outer_mom * mom_new + average)
    return (mom_new, glob_new)


def shape(rows, cols, dtype=jnp.bfloat16):
    return jax.ShapeDtypeStruct((rows, cols), dtype)


SMALL = pl.CostEstimate(flops=1, bytes_accessed=1, transcendentals=0)


def here():
    device = lax.axis_index("fsdp")
    return device // (2 * NY), lax.rem(device // 2, NY), lax.rem(device, 2)


def column(x, y, c):
    return pl.ds(pl.multiple_of(((x * NY + y) * 2 + c) * ROWS, ROWS), ROWS)


def pieces_of(tokens, up, wanted):
    groups = [(i, g) for i, stack in enumerate(wanted) for g in stack]

    def kernel(source, up_ref, *refs):
        targets, sems = refs[:-1], refs[-1]
        x, _, c = here()
        copies, filled = [], [0] * len(wanted)
        for n, (i, (dx, dc, start, size, with_up)) in enumerate(groups):
            rows, into = pl.ds(start, size), pl.ds(filled[i], size)
            filled[i] += size
            moves = [
                (
                    source.at[rows, column(1 - x if dx else x, k, 1 - c if dc else c)],
                    targets[i].at[into, pl.ds(k * ROWS, ROWS)],
                )
                for k in range(NY)
            ]
            if with_up:
                moves.append((up_ref.at[rows], targets[i].at[into, pl.ds(PIECE, F)]))
            for k, (here_from, here_to) in enumerate(moves):
                copies.append(pltpu.make_async_copy(here_from, here_to, sems.at[n, k]))
        for copy in copies:
            copy.start()
        for copy in copies:
            copy.wait()

    return pl.pallas_call(
        kernel,
        in_specs=[pl.BlockSpec(memory_space=pltpu.VMEM), pl.BlockSpec(memory_space=pltpu.HBM)],
        out_specs=[pl.BlockSpec(memory_space=pltpu.VMEM)] * len(wanted),
        out_shape=[
            shape(sum(g[3] for g in stack), PIECE + F * stack[0][4]) for stack in wanted
        ],
        scratch_shapes=[pltpu.SemaphoreType.DMA((len(groups), NY + 1))],
        cost_estimate=SMALL,
        compiler_params=VMEM,
        name="pieces",
    )(tokens, up)


def places(blocks):
    y = here()[1]
    for (step, start), block in zip(((0, 0), (1, 0), (3, 0), (2, 0), (2, HALF)), blocks, strict=True):
        at = pl.multiple_of(lax.rem(y + step, NY) * ROWS + start, HALF)
        yield pl.ds(at, block.shape[0]), block


def input_grad(ups, blocks):
    def kernel(u0, u1, u2, *refs):
        up = jnp.concatenate([u0[...], u1[...], u2[...]], axis=0)
        for at, block in places(refs[:5]):
            grad = lax.dot_general(
                up, block[...], (((1,), (1,)), ((), ())), preferred_element_type=jnp.float32
            )
            grad = (grad * SCALE).astype(jnp.bfloat16)
            for k, out in enumerate(refs[5:]):
                out[:, at] = grad[k * TOK : (k + 1) * TOK]

    return pl.pallas_call(
        kernel,
        in_specs=[pl.BlockSpec(memory_space=pltpu.VMEM)] * 8,
        out_specs=[pl.BlockSpec(memory_space=pltpu.VMEM)] * 4,
        out_shape=[shape(TOK, PIECE)] * 4,
        cost_estimate=SMALL,
        compiler_params=VMEM,
        name="input_grad",
    )(*ups, *blocks)


def value_parts(toks, blocks):
    def kernel(t0, t1, t2, t3, *refs):
        own, far, pair = refs[5:]
        total = jnp.zeros((4 * TOK, F), jnp.float32)
        for at, block in places(refs[:5]):
            tok = jnp.concatenate([t0[:, at], t1[:, at], t2[:, at], t3[:, at]], axis=0)
            total += jnp.dot(tok, block[...], preferred_element_type=jnp.float32)
        own[...] = total[:TOK]
        far[...] = total[TOK : 2 * TOK]
        pair[...] = total[2 * TOK :].astype(jnp.bfloat16)

    return pl.pallas_call(
        kernel,
        in_specs=[pl.BlockSpec(memory_space=pltpu.VMEM)] * 9,
        out_specs=[pl.BlockSpec(memory_space=pltpu.VMEM)] * 3,
        out_shape=[shape(TOK, F, jnp.float32)] * 2 + [shape(2 * TOK, F)],
        cost_estimate=SMALL,
        compiler_params=VMEM,
        name="values",
    )(*toks, *blocks)


def split(passed):
    def kernel(passed, out):
        out[...] = passed[:FIRST]

    return pl.pallas_call(
        kernel,
        in_specs=[pl.BlockSpec(memory_space=pltpu.VMEM)],
        out_specs=pl.BlockSpec(memory_space=pltpu.VMEM),
        out_shape=shape(FIRST, PIECE),
        cost_estimate=SMALL,
        compiler_params=VMEM,
        name="split",
    )(passed)


def pack(passed, val_back, val_x):
    rest = TOK - FIRST

    def kernel(passed, val_back, val_x, out):
        out[:rest] = passed[FIRST:]
        total = val_x[...] + val_back[TOK:].astype(jnp.float32)
        for k in range(NY):
            rows = slice(k * rest, (k + 1) * rest)
            out[rest:, k * F : (k + 1) * F] = total[rows].astype(jnp.bfloat16)

    return pl.pallas_call(
        kernel,
        in_specs=[pl.BlockSpec(memory_space=pltpu.VMEM)] * 3,
        out_specs=pl.BlockSpec(memory_space=pltpu.VMEM),
        out_shape=shape(2 * rest, PIECE),
        cost_estimate=SMALL,
        compiler_params=VMEM,
        name="pack",
    )(passed, val_back, val_x)


def weight_grad(toks, ups):
    def kernel(t0, t1, t2, t3, u0, u1, u2, own, to_above, to_below, keep_above, keep_below):
        up = jnp.concatenate([u0[...], u1[...], u2[...]], axis=0)
        y = here()[1]

        def block(step):
            at = pl.ds(pl.multiple_of(lax.rem(y + step, NY) * ROWS, ROWS), ROWS)
            tok = jnp.concatenate([t0[:, at], t1[:, at], t2[:, at], t3[:, at]], axis=0)
            return SCALE * lax.dot_general(
                tok, up, (((0,), (0,)), ((), ())), preferred_element_type=jnp.float32
            )

        grad = block(2)
        to_above[:HALF] = grad[:HALF].astype(jnp.bfloat16)
        to_below[:HALF] = grad[HALF:].astype(jnp.bfloat16)
        grad = block(1)
        keep_above[...] = grad[:LATER]
        to_above[HALF:] = grad[LATER:].astype(jnp.bfloat16)
        grad = block(3)
        to_below[HALF:] = grad[: ROWS - LATER].astype(jnp.bfloat16)
        keep_below[...] = grad[ROWS - LATER :]
        own[...] = block(0)

    return pl.pallas_call(
        kernel,
        in_specs=[pl.BlockSpec(memory_space=pltpu.VMEM)] * 7,
        out_specs=[pl.BlockSpec(memory_space=pltpu.VMEM)] * 5,
        out_shape=[shape(ROWS, F, jnp.float32)]
        + [shape(HALF + ROWS - LATER, F)] * 2
        + [shape(LATER, F, jnp.float32)] * 2,
        cost_estimate=SMALL,
        compiler_params=VMEM,
        name="weight_grad",
    )(*toks, *ups)


def relay(keep_above, keep_below, from_below, from_above):
    def kernel(keep_above, keep_below, from_below, from_above, to_above, to_below):
        more = LATER - HALF
        came = from_below[:HALF].astype(jnp.float32)
        to_above[:HALF] = (keep_above[:HALF] + came).astype(jnp.bfloat16)
        to_above[HALF:] = keep_above[HALF:].astype(jnp.bfloat16)
        came = from_above[:HALF].astype(jnp.float32)
        to_below[:more] = keep_below[:more].astype(jnp.bfloat16)
        to_below[more:] = (keep_below[more:] + came).astype(jnp.bfloat16)

    return pl.pallas_call(
        kernel,
        in_specs=[pl.BlockSpec(memory_space=pltpu.VMEM)] * 4,
        out_specs=[pl.BlockSpec(memory_space=pltpu.VMEM)] * 2,
        out_shape=[shape(LATER, F)] * 2,
        cost_estimate=SMALL,
        compiler_params=VMEM,
        name="relay",
    )(keep_above, keep_below, from_below, from_above)


def assemble(block, parts, wanted, vals=()):
    n = len(wanted)

    def kernel(*refs):
        target, sems = refs[-3 if vals else -2], refs[-1]
        x, _, c = here()
        copies = []
        for i, (dx, dc, start, size) in enumerate(wanted):
            for k in range(NY):
                place = column(1 - x if dx else x, k, 1 - c if dc else c)
                copies.append(
                    pltpu.make_async_copy(
                        refs[i].at[pl.ds(0, size), pl.ds(k * ROWS, ROWS)],
                        target.at[pl.ds(start, size), place],
                        sems.at[i * NY + k],
                    )
                )
        for copy in copies:
            copy.start()
        if vals:
            own, pair = refs[n : n + 2]
            rest = TOK - FIRST
            total = own[...] + pair[:TOK].astype(jnp.float32)
            for k in range(NY):
                rows = slice(k * rest, (k + 1) * rest)
                came = refs[n - 1][rest:, k * F : (k + 1) * F].astype(jnp.float32)
                refs[-2][rows] = ((total[rows] + came) * SCALE).astype(jnp.bfloat16)
        for copy in copies:
            copy.wait()

    args = [*parts, *vals]
    ins = [pl.BlockSpec(memory_space=pltpu.VMEM)] * len(args)
    outs, shapes, alias = [pl.BlockSpec(memory_space=pltpu.HBM)], [shape(TOK, D)], {}
    if vals:
        outs.append(pl.BlockSpec(memory_space=pltpu.VMEM))
        shapes.append(shape(TOK, F))
    if block is not None:
        alias = {len(args): 0}
        ins.append(pl.BlockSpec(memory_space=pltpu.HBM))
        args.append(block)
    return pl.pallas_call(
        kernel,
        in_specs=ins,
        out_specs=outs if vals else outs[0],
        out_shape=shapes if vals else shapes[0],
        scratch_shapes=[pltpu.SemaphoreType.DMA((NY * n,))],
        input_output_aliases=alias,
        cost_estimate=SMALL,
        compiler_params=VMEM,
        name="assemble",
    )(*args)


STRIP = 64


def adam(frag_index, grads, adam_m, adam_v, master, new_global):
    def kernel(frag, g0, from_above, r1, from_below, r3, m, v, w, glob, hbm_w, hbm_m, hbm_v, new_w, new_m, new_v, sems):
        at = pl.ds(pl.multiple_of(frag[0] * 128, 128), 128)
        copies = []
        for k in range(ROWS // STRIP):
            rows = pl.ds(k * STRIP, STRIP)
            top = k * STRIP
            if top < LATER:
                grad = g0[rows, :] + r1[rows, :].astype(jnp.float32)
            else:
                came = from_below[pl.ds(HALF + top - LATER, STRIP), :]
                grad = g0[rows, :] + came.astype(jnp.float32)
            if top < ROWS - LATER:
                grad = grad + from_above[pl.ds(HALF + top, STRIP), :].astype(jnp.float32)
            else:
                came = r3[pl.ds(top - (ROWS - LATER), STRIP), :]
                grad = grad + came.astype(jnp.float32)
            mom = beta_first * m[rows, :] + (1.0 - beta_first) * grad
            var = beta_second * v[rows, :] + (1.0 - beta_second) * grad * grad
            new_m[rows, :] = mom
            new_v[rows, :] = var
            old = w[rows, :]
            new_w[rows, :] = old - inner_rate * (
                mom / (jnp.sqrt(var) + epsilon) + decay_rate * old
            )
            new_w[rows, at] = mix_share * new_w[rows, at] + (1.0 - mix_share) * glob[rows, :]
            for i, (source, target) in enumerate(
                ((new_w, hbm_w), (new_m, hbm_m), (new_v, hbm_v))
            ):
                copy = pltpu.make_async_copy(source.at[rows], target.at[rows], sems.at[i, k])
                copy.start()
                copies.append(copy)
        for copy in copies:
            copy.wait()

    return pl.pallas_call(
        kernel,
        in_specs=[pl.BlockSpec(memory_space=pltpu.SMEM)]
        + [pl.BlockSpec(memory_space=pltpu.VMEM)] * 9,
        out_specs=[pl.BlockSpec(memory_space=pltpu.HBM)] * 3,
        out_shape=[shape(ROWS, F, jnp.float32)] * 3,
        scratch_shapes=[pltpu.VMEM((ROWS, F), jnp.float32)] * 3
        + [pltpu.SemaphoreType.DMA((3, ROWS // STRIP))],
        cost_estimate=SMALL,
        compiler_params=VMEM,
        name="adam",
    )(frag_index, *grads, adam_m, adam_v, master, new_global)


def body(
    token_in, cotangent, weight, adam_m, adam_v, pseudo_grad, momentum, global_frag, frag_index
):
    tokens = token_in[0]
    up_own = cotangent[0]
    master = weight[0]

    send_x, send_far = pieces_of(tokens, up_own, [((1, 0, 0, TOK, 1),), ((1, 1, 0, TOK, 0),)])
    tok_x = swap_x(send_x)
    for_far = swap_core(send_far)
    tok_far = swap_x(for_far)
    weight_bf = after(master.astype(jnp.bfloat16), send_x)
    block_1 = shift_y(weight_bf, -1)
    block_3 = shift_y(weight_bf, 1)
    tok_own, send_core = pieces_of(
        after(tokens, send_x), up_own, [((0, 0, 0, TOK, 0),), ((0, 1, 0, TOK, 0),)]
    )
    tok_core = swap_core(send_core)
    up_x = tok_x[:, PIECE:]
    up_pair = swap_core(jnp.concatenate([up_own, up_x]))
    block_2a = shift_y(block_1[:HALF], -1)
    block_2b = shift_y(block_3[HALF:], 1)
    blocks = (weight_bf, block_1, block_3, block_2a, block_2b)

    total = replica_step(after(pseudo_grad[0].astype(jnp.bfloat16), tok_core, for_far), lambda i: i ^ 6)
    total = replica_step(total, lambda i: i ^ 1)
    up_ready, total = lax.optimization_barrier((up_own, total))
    toks = (tok_own, tok_x, tok_core, tok_far)
    g0, to_above, to_below, keep_above, keep_below = weight_grad(toks, (up_ready, up_x, up_pair))
    from_below, from_above = shift_y(to_above, 1), shift_y(to_below, -1)

    ig_own, ig_x, ig_core, ig_far = input_grad((after(up_ready, g0), up_x, up_pair), blocks)
    back_x = swap_x(ig_x)
    back_far = swap_core(ig_far)
    back_core = swap_core(ig_core)
    other_a = swap_x(split(back_far))

    val_own, val_x, val_pair = value_parts(toks, (after(weight_bf, g0), *blocks[1:]))
    val_back = swap_core(val_pair)
    other_b = swap_x(after(pack(back_far, val_back, val_x), other_a))
    total = replica_step(after(total, back_core), lambda i: i ^ 2)

    s1, s3 = relay(after(keep_above, back_x), keep_below, from_below, from_above)
    r1 = shift_y(s1, 1)
    r3 = shift_y(s3, -1)

    total = replica_step(after(total, s1), lambda i: i ^ 8)
    new_momentum, new_global = outer_update(momentum, global_frag, total / 16)

    block = assemble(
        None, (ig_own, back_core, back_x), ((0, 0, 0, TOK), (0, 1, 0, TOK), (1, 0, 0, TOK))
    )
    new_weight, new_m, new_v = adam(
        frag_index, (g0, from_above, r1, from_below, r3), adam_m[0], adam_v[0], master, new_global
    )
    other_b = after(other_b, new_weight)
    block, values = assemble(
        block, (other_a, other_b), ((1, 1, 0, FIRST), (1, 1, FIRST, TOK - FIRST)), (val_own, val_back)
    )
    return (
        values[None],
        block[None],
        new_weight[None],
        new_m[None],
        new_v[None],
        new_global,
        new_momentum,
    )


def solution(mesh):
    in_specs = (
        P("replica", "fsdp", None),
        P("replica", "fsdp", None),
        P("replica", "fsdp", None),
        P("replica", "fsdp", None),
        P("replica", "fsdp", None),
        P("replica", "fsdp", None),
        P("fsdp", None),
        P("fsdp", None),
        P(),
    )
    out_specs = (
        P("replica", "fsdp", None),
        P("replica", "fsdp", None),
        P("replica", "fsdp", None),
        P("replica", "fsdp", None),
        P("replica", "fsdp", None),
        P("fsdp", None),
        P("fsdp", None),
    )
    return jax.shard_map(body, mesh=mesh, in_specs=in_specs, out_specs=out_specs, check_vma=False)
```

```python
import functools

import jax
import jax.numpy as jnp
from jax import lax
from jax.experimental import pallas as pl
from jax.experimental.pallas import tpu as pltpu
from jax.sharding import PartitionSpec as P

D = 8192
SCALE = D ** (-0.5)

beta_first = 0.9
beta_second = 0.95
epsilon = 1e-08
inner_rate = 0.01
decay_rate = 0.1
outer_rate = 0.7
outer_mom = 0.9
mix_share = 0.5

NY = 4
TOK = 128
ROWS = 512
F = 512
PIECE = NY * ROWS
HALF = ROWS // 2
FIRST = 96
LATER = 320
VMEM = pltpu.CompilerParams(vmem_limit_bytes=40 * 1024 * 1024)


def fsdp_permute(value, target):
    pairs = []
    for i in range(16):
        x, y, c = i // 8, (i // 2) % NY, i % 2
        x2, y2, c2 = target(x, y, c)
        pairs.append((i, ((x2 % 2) * NY + y2 % NY) * 2 + c2 % 2))
    return lax.ppermute(value, "fsdp", pairs)


def swap_x(value):
    return fsdp_permute(value, lambda x, y, c: (x + 1, y, c))


def swap_core(value):
    return fsdp_permute(value, lambda x, y, c: (x, y, c + 1))


def shift_y(value, step):
    return fsdp_permute(value, lambda x, y, c: (x, y + step, c))


def replica_step(total, partner):
    sent = total.astype(jnp.bfloat16)
    other = lax.ppermute(sent, "replica", [(i, partner(i)) for i in range(16)])
    return sent.astype(jnp.float32) + other.astype(jnp.float32)


def after(value, *others):
    return lax.optimization_barrier((value, *others))[0]


def outer_update(momentum, global_frag, average):
    mom_new = outer_mom * momentum + average
    glob_new = global_frag - outer_rate * (outer_mom * mom_new + average)
    return (mom_new, glob_new)


def shape(rows, cols, dtype=jnp.bfloat16):
    return jax.ShapeDtypeStruct((rows, cols), dtype)


SMALL = pl.CostEstimate(flops=1, bytes_accessed=1, transcendentals=0)


def here():
    device = lax.axis_index("fsdp")
    return device // (2 * NY), lax.rem(device // 2, NY), lax.rem(device, 2)


def column(x, y, c):
    return pl.ds(pl.multiple_of(((x * NY + y) * 2 + c) * ROWS, ROWS), ROWS)


def pieces_of(tokens, up, wanted):
    groups = [(i, g) for i, stack in enumerate(wanted) for g in stack]

    def kernel(source, up_ref, *refs):
        targets, sems = refs[:-1], refs[-1]
        x, _, c = here()
        copies, filled = [], [0] * len(wanted)
        for n, (i, (dx, dc, start, size, with_up)) in enumerate(groups):
            rows, into = pl.ds(start, size), pl.ds(filled[i], size)
            filled[i] += size
            moves = [
                (
                    source.at[rows, column(1 - x if dx else x, k, 1 - c if dc else c)],
                    targets[i].at[into, pl.ds(k * ROWS, ROWS)],
                )
                for k in range(NY)
            ]
            if with_up:
                moves.append((up_ref.at[rows], targets[i].at[into, pl.ds(PIECE, F)]))
            for k, (here_from, here_to) in enumerate(moves):
                copies.append(pltpu.make_async_copy(here_from, here_to, sems.at[n, k]))
        for copy in copies:
            copy.start()
        for copy in copies:
            copy.wait()

    return pl.pallas_call(
        kernel,
        in_specs=[pl.BlockSpec(memory_space=pltpu.VMEM), pl.BlockSpec(memory_space=pltpu.HBM)],
        out_specs=[pl.BlockSpec(memory_space=pltpu.VMEM)] * len(wanted),
        out_shape=[
            shape(sum(g[3] for g in stack), PIECE + F * stack[0][4]) for stack in wanted
        ],
        scratch_shapes=[pltpu.SemaphoreType.DMA((len(groups), NY + 1))],
        cost_estimate=SMALL,
        compiler_params=VMEM,
        name="pieces",
    )(tokens, up)


def places(blocks):
    y = here()[1]
    for (step, start), block in zip(((0, 0), (1, 0), (3, 0), (2, 0), (2, HALF)), blocks, strict=True):
        at = pl.multiple_of(lax.rem(y + step, NY) * ROWS + start, HALF)
        yield pl.ds(at, block.shape[0]), block


def input_grad(ups, blocks):
    def kernel(u0, u1, u2, *refs):
        up = jnp.concatenate([u0[...], u1[...], u2[...]], axis=0)
        for at, block in places(refs[:5]):
            grad = lax.dot_general(
                up, block[...], (((1,), (1,)), ((), ())), preferred_element_type=jnp.float32
            )
            grad = (grad * SCALE).astype(jnp.bfloat16)
            for k, out in enumerate(refs[5:]):
                out[:, at] = grad[k * TOK : (k + 1) * TOK]

    return pl.pallas_call(
        kernel,
        in_specs=[pl.BlockSpec(memory_space=pltpu.VMEM)] * 8,
        out_specs=[pl.BlockSpec(memory_space=pltpu.VMEM)] * 4,
        out_shape=[shape(TOK, PIECE)] * 4,
        cost_estimate=SMALL,
        compiler_params=VMEM,
        name="input_grad",
    )(*ups, *blocks)


def value_parts(toks, blocks):
    def kernel(t0, t1, t2, t3, *refs):
        own, far, pair = refs[5:]
        total = jnp.zeros((4 * TOK, F), jnp.float32)
        for at, block in places(refs[:5]):
            tok = jnp.concatenate([t0[:, at], t1[:, at], t2[:, at], t3[:, at]], axis=0)
            total += jnp.dot(tok, block[...], preferred_element_type=jnp.float32)
        own[...] = total[:TOK]
        far[...] = total[TOK : 2 * TOK]
        pair[...] = total[2 * TOK :].astype(jnp.bfloat16)

    return pl.pallas_call(
        kernel,
        in_specs=[pl.BlockSpec(memory_space=pltpu.VMEM)] * 9,
        out_specs=[pl.BlockSpec(memory_space=pltpu.VMEM)] * 3,
        out_shape=[shape(TOK, F, jnp.float32)] * 2 + [shape(2 * TOK, F)],
        cost_estimate=SMALL,
        compiler_params=VMEM,
        name="values",
    )(*toks, *blocks)


def split(passed):
    def kernel(passed, out):
        out[...] = passed[:FIRST]

    return pl.pallas_call(
        kernel,
        in_specs=[pl.BlockSpec(memory_space=pltpu.VMEM)],
        out_specs=pl.BlockSpec(memory_space=pltpu.VMEM),
        out_shape=shape(FIRST, PIECE),
        cost_estimate=SMALL,
        compiler_params=VMEM,
        name="split",
    )(passed)


def pack(passed, val_back, val_x):
    rest = TOK - FIRST

    def kernel(passed, val_back, val_x, out):
        out[:rest] = passed[FIRST:]
        total = val_x[...] + val_back[TOK:].astype(jnp.float32)
        for k in range(NY):
            rows = slice(k * rest, (k + 1) * rest)
            out[rest:, k * F : (k + 1) * F] = total[rows].astype(jnp.bfloat16)

    return pl.pallas_call(
        kernel,
        in_specs=[pl.BlockSpec(memory_space=pltpu.VMEM)] * 3,
        out_specs=pl.BlockSpec(memory_space=pltpu.VMEM),
        out_shape=shape(2 * rest, PIECE),
        cost_estimate=SMALL,
        compiler_params=VMEM,
        name="pack",
    )(passed, val_back, val_x)


def weight_grad(toks, ups):
    def kernel(t0, t1, t2, t3, u0, u1, u2, own, to_above, to_below, keep_above, keep_below):
        up = jnp.concatenate([u0[...], u1[...], u2[...]], axis=0)
        y = here()[1]

        def block(step):
            at = pl.ds(pl.multiple_of(lax.rem(y + step, NY) * ROWS, ROWS), ROWS)
            tok = jnp.concatenate([t0[:, at], t1[:, at], t2[:, at], t3[:, at]], axis=0)
            return SCALE * lax.dot_general(
                tok, up, (((0,), (0,)), ((), ())), preferred_element_type=jnp.float32
            )

        grad = block(2)
        to_above[:HALF] = grad[:HALF].astype(jnp.bfloat16)
        to_below[:HALF] = grad[HALF:].astype(jnp.bfloat16)
        grad = block(1)
        keep_above[...] = grad[:LATER]
        to_above[HALF:] = grad[LATER:].astype(jnp.bfloat16)
        grad = block(3)
        to_below[HALF:] = grad[: ROWS - LATER].astype(jnp.bfloat16)
        keep_below[...] = grad[ROWS - LATER :]
        own[...] = block(0)

    return pl.pallas_call(
        kernel,
        in_specs=[pl.BlockSpec(memory_space=pltpu.VMEM)] * 7,
        out_specs=[pl.BlockSpec(memory_space=pltpu.VMEM)] * 5,
        out_shape=[shape(ROWS, F, jnp.float32)]
        + [shape(HALF + ROWS - LATER, F)] * 2
        + [shape(LATER, F, jnp.float32)] * 2,
        cost_estimate=SMALL,
        compiler_params=VMEM,
        name="weight_grad",
    )(*toks, *ups)


def relay(keep_above, keep_below, from_below, from_above):
    def kernel(keep_above, keep_below, from_below, from_above, to_above, to_below):
        more = LATER - HALF
        came = from_below[:HALF].astype(jnp.float32)
        to_above[:HALF] = (keep_above[:HALF] + came).astype(jnp.bfloat16)
        to_above[HALF:] = keep_above[HALF:].astype(jnp.bfloat16)
        came = from_above[:HALF].astype(jnp.float32)
        to_below[:more] = keep_below[:more].astype(jnp.bfloat16)
        to_below[more:] = (keep_below[more:] + came).astype(jnp.bfloat16)

    return pl.pallas_call(
        kernel,
        in_specs=[pl.BlockSpec(memory_space=pltpu.VMEM)] * 4,
        out_specs=[pl.BlockSpec(memory_space=pltpu.VMEM)] * 2,
        out_shape=[shape(LATER, F)] * 2,
        cost_estimate=SMALL,
        compiler_params=VMEM,
        name="relay",
    )(keep_above, keep_below, from_below, from_above)


def assemble(block, parts, wanted, vals=()):
    n = len(wanted)

    def kernel(*refs):
        target, sems = refs[-3 if vals else -2], refs[-1]
        x, _, c = here()
        copies = []
        for i, (dx, dc, start, size) in enumerate(wanted):
            for k in range(NY):
                place = column(1 - x if dx else x, k, 1 - c if dc else c)
                copies.append(
                    pltpu.make_async_copy(
                        refs[i].at[pl.ds(0, size), pl.ds(k * ROWS, ROWS)],
                        target.at[pl.ds(start, size), place],
                        sems.at[i * NY + k],
                    )
                )
        for copy in copies:
            copy.start()
        if vals:
            own, pair = refs[n : n + 2]
            rest = TOK - FIRST
            total = own[...] + pair[:TOK].astype(jnp.float32)
            for k in range(NY):
                rows = slice(k * rest, (k + 1) * rest)
                came = refs[n - 1][rest:, k * F : (k + 1) * F].astype(jnp.float32)
                refs[-2][rows] = ((total[rows] + came) * SCALE).astype(jnp.bfloat16)
        for copy in copies:
            copy.wait()

    args = [*parts, *vals]
    ins = [pl.BlockSpec(memory_space=pltpu.VMEM)] * len(args)
    outs, shapes, alias = [pl.BlockSpec(memory_space=pltpu.HBM)], [shape(TOK, D)], {}
    if vals:
        outs.append(pl.BlockSpec(memory_space=pltpu.VMEM))
        shapes.append(shape(TOK, F))
    if block is not None:
        alias = {len(args): 0}
        ins.append(pl.BlockSpec(memory_space=pltpu.HBM))
        args.append(block)
    return pl.pallas_call(
        kernel,
        in_specs=ins,
        out_specs=outs if vals else outs[0],
        out_shape=shapes if vals else shapes[0],
        scratch_shapes=[pltpu.SemaphoreType.DMA((NY * n,))],
        input_output_aliases=alias,
        cost_estimate=SMALL,
        compiler_params=VMEM,
        name="assemble",
    )(*args)


STRIP = 64


def adam(frag_index, grads, adam_m, adam_v, master, new_global):
    def kernel(frag, g0, from_above, r1, from_below, r3, m, v, w, glob, hbm_w, hbm_m, hbm_v, new_w, new_m, new_v, sems):
        at = pl.ds(pl.multiple_of(frag[0] * 128, 128), 128)
        copies = []
        for k in range(ROWS // STRIP):
            rows = pl.ds(k * STRIP, STRIP)
            top = k * STRIP
            if top < LATER:
                grad = g0[rows, :] + r1[rows, :].astype(jnp.float32)
            else:
                came = from_below[pl.ds(HALF + top - LATER, STRIP), :]
                grad = g0[rows, :] + came.astype(jnp.float32)
            if top < ROWS - LATER:
                grad = grad + from_above[pl.ds(HALF + top, STRIP), :].astype(jnp.float32)
            else:
                came = r3[pl.ds(top - (ROWS - LATER), STRIP), :]
                grad = grad + came.astype(jnp.float32)
            mom = beta_first * m[rows, :] + (1.0 - beta_first) * grad
            var = beta_second * v[rows, :] + (1.0 - beta_second) * grad * grad
            new_m[rows, :] = mom
            new_v[rows, :] = var
            old = w[rows, :]
            new_w[rows, :] = old - inner_rate * (
                mom / (jnp.sqrt(var) + epsilon) + decay_rate * old
            )
            new_w[rows, at] = mix_share * new_w[rows, at] + (1.0 - mix_share) * glob[rows, :]
            for i, (source, target) in enumerate(
                ((new_w, hbm_w), (new_m, hbm_m), (new_v, hbm_v))
            ):
                copy = pltpu.make_async_copy(source.at[rows], target.at[rows], sems.at[i, k])
                copy.start()
                copies.append(copy)
        for copy in copies:
            copy.wait()

    return pl.pallas_call(
        kernel,
        in_specs=[pl.BlockSpec(memory_space=pltpu.SMEM)]
        + [pl.BlockSpec(memory_space=pltpu.VMEM)] * 9,
        out_specs=[pl.BlockSpec(memory_space=pltpu.HBM)] * 3,
        out_shape=[shape(ROWS, F, jnp.float32)] * 3,
        scratch_shapes=[pltpu.VMEM((ROWS, F), jnp.float32)] * 3
        + [pltpu.SemaphoreType.DMA((3, ROWS // STRIP))],
        cost_estimate=SMALL,
        compiler_params=VMEM,
        name="adam",
    )(frag_index, *grads, adam_m, adam_v, master, new_global)


def body(
    token_in, cotangent, weight, adam_m, adam_v, pseudo_grad, momentum, global_frag, frag_index
):
    tokens = token_in[0]
    up_own = cotangent[0]
    master = weight[0]

    send_x, send_far = pieces_of(tokens, up_own, [((1, 0, 0, TOK, 1),), ((1, 1, 0, TOK, 0),)])
    tok_x = swap_x(send_x)
    for_far = swap_core(send_far)
    tok_far = swap_x(for_far)
    weight_bf = after(master.astype(jnp.bfloat16), for_far)
    block_1 = shift_y(weight_bf, -1)
    block_3 = shift_y(weight_bf, 1)
    tok_own, send_core = pieces_of(
        after(tokens, send_x), up_own, [((0, 0, 0, TOK, 0),), ((0, 1, 0, TOK, 0),)]
    )
    tok_core = swap_core(send_core)
    up_x = tok_x[:, PIECE:]
    up_pair = swap_core(jnp.concatenate([up_own, up_x]))
    block_2a = shift_y(block_1[:HALF], -1)
    block_2b = shift_y(block_3[HALF:], 1)
    blocks = (weight_bf, block_1, block_3, block_2a, block_2b)

    total = replica_step(after(pseudo_grad[0].astype(jnp.bfloat16), tok_core, for_far), lambda i: i ^ 6)
    total = replica_step(total, lambda i: i ^ 1)
    up_ready, total = lax.optimization_barrier((up_own, total))
    toks = (tok_own, tok_x, tok_core, tok_far)
    ig_own, ig_x, ig_core, ig_far = input_grad((up_ready, up_x, up_pair), blocks)
    back_x = swap_x(ig_x)
    back_far = swap_core(ig_far)
    back_core = swap_core(ig_core)
    other_a = swap_x(split(back_far))

    g0, to_above, to_below, keep_above, keep_below = weight_grad(
        toks, (after(up_own, ig_own), up_x, up_pair)
    )
    from_below, from_above = shift_y(to_above, 1), shift_y(to_below, -1)

    val_own, val_x, val_pair = value_parts(toks, (after(weight_bf, g0), *blocks[1:]))
    val_back = swap_core(val_pair)
    other_b = swap_x(after(pack(back_far, val_back, val_x), other_a))
    total = replica_step(after(total, back_core), lambda i: i ^ 2)

    s1, s3 = relay(after(keep_above, back_x), keep_below, from_below, from_above)
    r1 = shift_y(s1, 1)
    r3 = shift_y(s3, -1)

    total = replica_step(after(total, s1), lambda i: i ^ 8)
    new_momentum, new_global = outer_update(momentum, global_frag, total / 16)

    block = assemble(
        None, (ig_own, back_core, back_x), ((0, 0, 0, TOK), (0, 1, 0, TOK), (1, 0, 0, TOK))
    )
    new_weight, new_m, new_v = adam(
        frag_index, (g0, from_above, r1, from_below, r3), adam_m[0], adam_v[0], master, new_global
    )
    other_b = after(other_b, new_weight)
    block, values = assemble(
        block, (other_a, other_b), ((1, 1, 0, FIRST), (1, 1, FIRST, TOK - FIRST)), (val_own, val_back)
    )
    return (
        values[None],
        block[None],
        new_weight[None],
        new_m[None],
        new_v[None],
        new_global,
        new_momentum,
    )


def solution(mesh):
    in_specs = (
        P("replica", "fsdp", None),
        P("replica", "fsdp", None),
        P("replica", "fsdp", None),
        P("replica", "fsdp", None),
        P("replica", "fsdp", None),
        P("replica", "fsdp", None),
        P("fsdp", None),
        P("fsdp", None),
        P(),
    )
    out_specs = (
        P("replica", "fsdp", None),
        P("replica", "fsdp", None),
        P("replica", "fsdp", None),
        P("replica", "fsdp", None),
        P("replica", "fsdp", None),
        P("fsdp", None),
        P("fsdp", None),
    )
    return jax.shard_map(body, mesh=mesh, in_specs=in_specs, out_specs=out_specs, check_vma=False)
```

```python
import functools

import jax
import jax.numpy as jnp
from jax import lax
from jax.experimental import pallas as pl
from jax.experimental.pallas import tpu as pltpu
from jax.sharding import PartitionSpec as P

D = 8192
SCALE = D ** (-0.5)

beta_first = 0.9
beta_second = 0.95
epsilon = 1e-08
inner_rate = 0.01
decay_rate = 0.1
outer_rate = 0.7
outer_mom = 0.9
mix_share = 0.5

NY = 4
TOK = 128
ROWS = 512
F = 512
PIECE = NY * ROWS
HALF = ROWS // 2
FIRST = 96
LATER = 320
VMEM = pltpu.CompilerParams(vmem_limit_bytes=40 * 1024 * 1024)


def fsdp_permute(value, target):
    pairs = []
    for i in range(16):
        x, y, c = i // 8, (i // 2) % NY, i % 2
        x2, y2, c2 = target(x, y, c)
        pairs.append((i, ((x2 % 2) * NY + y2 % NY) * 2 + c2 % 2))
    return lax.ppermute(value, "fsdp", pairs)


def swap_x(value):
    return fsdp_permute(value, lambda x, y, c: (x + 1, y, c))


def swap_core(value):
    return fsdp_permute(value, lambda x, y, c: (x, y, c + 1))


def shift_y(value, step):
    return fsdp_permute(value, lambda x, y, c: (x, y + step, c))


def replica_step(total, partner):
    sent = total.astype(jnp.bfloat16)
    other = lax.ppermute(sent, "replica", [(i, partner(i)) for i in range(16)])
    return sent.astype(jnp.float32) + other.astype(jnp.float32)


def after(value, *others):
    return lax.optimization_barrier((value, *others))[0]


def outer_update(momentum, global_frag, average):
    mom_new = outer_mom * momentum + average
    glob_new = global_frag - outer_rate * (outer_mom * mom_new + average)
    return (mom_new, glob_new)


def shape(rows, cols, dtype=jnp.bfloat16):
    return jax.ShapeDtypeStruct((rows, cols), dtype)


SMALL = pl.CostEstimate(flops=1, bytes_accessed=1, transcendentals=0)


def here():
    device = lax.axis_index("fsdp")
    return device // (2 * NY), lax.rem(device // 2, NY), lax.rem(device, 2)


def column(x, y, c):
    return pl.ds(pl.multiple_of(((x * NY + y) * 2 + c) * ROWS, ROWS), ROWS)


def pieces_of(tokens, up, wanted):
    groups = [(i, g) for i, stack in enumerate(wanted) for g in stack]

    def kernel(source, up_ref, *refs):
        targets, sems = refs[:-1], refs[-1]
        x, _, c = here()
        copies, filled = [], [0] * len(wanted)
        for n, (i, (dx, dc, start, size, with_up)) in enumerate(groups):
            rows, into = pl.ds(start, size), pl.ds(filled[i], size)
            filled[i] += size
            moves = [
                (
                    source.at[rows, column(1 - x if dx else x, k, 1 - c if dc else c)],
                    targets[i].at[into, pl.ds(k * ROWS, ROWS)],
                )
                for k in range(NY)
            ]
            if with_up:
                moves.append((up_ref.at[rows], targets[i].at[into, pl.ds(PIECE, F)]))
            for k, (here_from, here_to) in enumerate(moves):
                copies.append(pltpu.make_async_copy(here_from, here_to, sems.at[n, k]))
        for copy in copies:
            copy.start()
        for copy in copies:
            copy.wait()

    return pl.pallas_call(
        kernel,
        in_specs=[pl.BlockSpec(memory_space=pltpu.VMEM), pl.BlockSpec(memory_space=pltpu.HBM)],
        out_specs=[pl.BlockSpec(memory_space=pltpu.VMEM)] * len(wanted),
        out_shape=[
            shape(sum(g[3] for g in stack), PIECE + F * stack[0][4]) for stack in wanted
        ],
        scratch_shapes=[pltpu.SemaphoreType.DMA((len(groups), NY + 1))],
        cost_estimate=SMALL,
        compiler_params=VMEM,
        name="pieces",
    )(tokens, up)


def places(blocks):
    y = here()[1]
    for (step, start), block in zip(((0, 0), (1, 0), (3, 0), (2, 0), (2, HALF)), blocks, strict=True):
        at = pl.multiple_of(lax.rem(y + step, NY) * ROWS + start, HALF)
        yield pl.ds(at, block.shape[0]), block


def input_grad(ups, blocks):
    def kernel(u0, u1, u2, *refs):
        up = jnp.concatenate([u0[...], u1[...], u2[...]], axis=0)
        for at, block in places(refs[:5]):
            grad = lax.dot_general(
                up, block[...], (((1,), (1,)), ((), ())), preferred_element_type=jnp.float32
            )
            grad = (grad * SCALE).astype(jnp.bfloat16)
            for k, out in enumerate(refs[5:]):
                out[:, at] = grad[k * TOK : (k + 1) * TOK]

    return pl.pallas_call(
        kernel,
        in_specs=[pl.BlockSpec(memory_space=pltpu.VMEM)] * 8,
        out_specs=[pl.BlockSpec(memory_space=pltpu.VMEM)] * 4,
        out_shape=[shape(TOK, PIECE)] * 4,
        cost_estimate=SMALL,
        compiler_params=VMEM,
        name="input_grad",
    )(*ups, *blocks)


def value_parts(toks, blocks):
    def kernel(t0, t1, t2, t3, *refs):
        own, far, pair = refs[5:]
        total = jnp.zeros((4 * TOK, F), jnp.float32)
        for at, block in places(refs[:5]):
            tok = jnp.concatenate([t0[:, at], t1[:, at], t2[:, at], t3[:, at]], axis=0)
            total += jnp.dot(tok, block[...], preferred_element_type=jnp.float32)
        own[...] = total[:TOK]
        far[...] = total[TOK : 2 * TOK]
        pair[...] = total[2 * TOK :].astype(jnp.bfloat16)

    return pl.pallas_call(
        kernel,
        in_specs=[pl.BlockSpec(memory_space=pltpu.VMEM)] * 9,
        out_specs=[pl.BlockSpec(memory_space=pltpu.VMEM)] * 3,
        out_shape=[shape(TOK, F, jnp.float32)] * 2 + [shape(2 * TOK, F)],
        cost_estimate=SMALL,
        compiler_params=VMEM,
        name="values",
    )(*toks, *blocks)


def split(passed):
    def kernel(passed, out):
        out[...] = passed[:FIRST]

    return pl.pallas_call(
        kernel,
        in_specs=[pl.BlockSpec(memory_space=pltpu.VMEM)],
        out_specs=pl.BlockSpec(memory_space=pltpu.VMEM),
        out_shape=shape(FIRST, PIECE),
        cost_estimate=SMALL,
        compiler_params=VMEM,
        name="split",
    )(passed)


def pack(passed, val_back, val_x):
    rest = TOK - FIRST

    def kernel(passed, val_back, val_x, out):
        out[:rest] = passed[FIRST:]
        total = val_x[...] + val_back[TOK:].astype(jnp.float32)
        for k in range(NY):
            rows = slice(k * rest, (k + 1) * rest)
            out[rest:, k * F : (k + 1) * F] = total[rows].astype(jnp.bfloat16)

    return pl.pallas_call(
        kernel,
        in_specs=[pl.BlockSpec(memory_space=pltpu.VMEM)] * 3,
        out_specs=pl.BlockSpec(memory_space=pltpu.VMEM),
        out_shape=shape(2 * rest, PIECE),
        cost_estimate=SMALL,
        compiler_params=VMEM,
        name="pack",
    )(passed, val_back, val_x)


def weight_grad(toks, ups):
    def kernel(t0, t1, t2, t3, u0, u1, u2, own, to_above, to_below, keep_above, keep_below):
        up = jnp.concatenate([u0[...], u1[...], u2[...]], axis=0)
        y = here()[1]

        def block(step):
            at = pl.ds(pl.multiple_of(lax.rem(y + step, NY) * ROWS, ROWS), ROWS)
            tok = jnp.concatenate([t0[:, at], t1[:, at], t2[:, at], t3[:, at]], axis=0)
            return SCALE * lax.dot_general(
                tok, up, (((0,), (0,)), ((), ())), preferred_element_type=jnp.float32
            )

        grad = block(2)
        to_above[:HALF] = grad[:HALF].astype(jnp.bfloat16)
        to_below[:HALF] = grad[HALF:].astype(jnp.bfloat16)
        grad = block(1)
        keep_above[...] = grad[:LATER]
        to_above[HALF:] = grad[LATER:].astype(jnp.bfloat16)
        grad = block(3)
        to_below[HALF:] = grad[: ROWS - LATER].astype(jnp.bfloat16)
        keep_below[...] = grad[ROWS - LATER :]
        own[...] = block(0)

    return pl.pallas_call(
        kernel,
        in_specs=[pl.BlockSpec(memory_space=pltpu.VMEM)] * 7,
        out_specs=[pl.BlockSpec(memory_space=pltpu.VMEM)] * 5,
        out_shape=[shape(ROWS, F, jnp.float32)]
        + [shape(HALF + ROWS - LATER, F)] * 2
        + [shape(LATER, F, jnp.float32)] * 2,
        cost_estimate=SMALL,
        compiler_params=VMEM,
        name="weight_grad",
    )(*toks, *ups)


def relay(keep_above, keep_below, from_below, from_above):
    def kernel(keep_above, keep_below, from_below, from_above, to_above, to_below):
        more = LATER - HALF
        came = from_below[:HALF].astype(jnp.float32)
        to_above[:HALF] = (keep_above[:HALF] + came).astype(jnp.bfloat16)
        to_above[HALF:] = keep_above[HALF:].astype(jnp.bfloat16)
        came = from_above[:HALF].astype(jnp.float32)
        to_below[:more] = keep_below[:more].astype(jnp.bfloat16)
        to_below[more:] = (keep_below[more:] + came).astype(jnp.bfloat16)

    return pl.pallas_call(
        kernel,
        in_specs=[pl.BlockSpec(memory_space=pltpu.VMEM)] * 4,
        out_specs=[pl.BlockSpec(memory_space=pltpu.VMEM)] * 2,
        out_shape=[shape(LATER, F)] * 2,
        cost_estimate=SMALL,
        compiler_params=VMEM,
        name="relay",
    )(keep_above, keep_below, from_below, from_above)


def assemble(block, parts, wanted, vals=()):
    n = len(wanted)

    def kernel(*refs):
        *_, target, sems = refs if not vals else (refs[-4], refs[-1])
        x, _, c = here()
        copies = []
        for i, (dx, dc, start, size) in enumerate(wanted):
            for k in range(NY):
                place = column(1 - x if dx else x, k, 1 - c if dc else c)
                copies.append(
                    pltpu.make_async_copy(
                        refs[i].at[pl.ds(0, size), pl.ds(k * ROWS, ROWS)],
                        target.at[pl.ds(start, size), place],
                        sems.at[i * NY + k],
                    )
                )
        for copy in copies:
            copy.start()
        if vals:
            own, pair = refs[n : n + 2]
            rest = TOK - FIRST
            total = own[...] + pair[:TOK].astype(jnp.float32)
            for k in range(NY):
                rows = slice(k * rest, (k + 1) * rest)
                came = refs[n - 1][rest:, k * F : (k + 1) * F].astype(jnp.float32)
                refs[-2][rows] = ((total[rows] + came) * SCALE).astype(jnp.bfloat16)
            copies.append(pltpu.make_async_copy(refs[-2], refs[-3], sems.at[NY * n]))
            copies[-1].start()
        for copy in copies:
            copy.wait()

    args = [*parts, *vals]
    ins = [pl.BlockSpec(memory_space=pltpu.VMEM)] * len(args)
    outs, shapes, alias = [pl.BlockSpec(memory_space=pltpu.HBM)], [shape(TOK, D)], {}
    if vals:
        outs.append(pl.BlockSpec(memory_space=pltpu.HBM))
        shapes.append(shape(TOK, F))
    if block is not None:
        alias = {len(args): 0}
        ins.append(pl.BlockSpec(memory_space=pltpu.HBM))
        args.append(block)
    return pl.pallas_call(
        kernel,
        in_specs=ins,
        out_specs=outs if vals else outs[0],
        out_shape=shapes if vals else shapes[0],
        scratch_shapes=[pltpu.VMEM((TOK, F), jnp.bfloat16)] * bool(vals)
        + [pltpu.SemaphoreType.DMA((NY * n + 1,))],
        input_output_aliases=alias,
        cost_estimate=SMALL,
        compiler_params=VMEM,
        name="assemble",
    )(*args)


STRIP = 64


def adam(frag_index, grads, adam_m, adam_v, master, new_global):
    def kernel(frag, g0, from_above, r1, from_below, r3, m, v, w, glob, hbm_w, hbm_m, hbm_v, new_w, new_m, new_v, sems):
        at = pl.ds(pl.multiple_of(frag[0] * 128, 128), 128)
        copies = []
        for k in range(ROWS // STRIP):
            rows = pl.ds(k * STRIP, STRIP)
            top = k * STRIP
            if top < LATER:
                grad = g0[rows, :] + r1[rows, :].astype(jnp.float32)
            else:
                came = from_below[pl.ds(HALF + top - LATER, STRIP), :]
                grad = g0[rows, :] + came.astype(jnp.float32)
            if top < ROWS - LATER:
                grad = grad + from_above[pl.ds(HALF + top, STRIP), :].astype(jnp.float32)
            else:
                came = r3[pl.ds(top - (ROWS - LATER), STRIP), :]
                grad = grad + came.astype(jnp.float32)
            mom = beta_first * m[rows, :] + (1.0 - beta_first) * grad
            var = beta_second * v[rows, :] + (1.0 - beta_second) * grad * grad
            new_m[rows, :] = mom
            new_v[rows, :] = var
            old = w[rows, :]
            new_w[rows, :] = old - inner_rate * (
                mom / (jnp.sqrt(var) + epsilon) + decay_rate * old
            )
            new_w[rows, at] = mix_share * new_w[rows, at] + (1.0 - mix_share) * glob[rows, :]
            for i, (source, target) in enumerate(
                ((new_w, hbm_w), (new_m, hbm_m), (new_v, hbm_v))
            ):
                copy = pltpu.make_async_copy(source.at[rows], target.at[rows], sems.at[i, k])
                copy.start()
                copies.append(copy)
        for copy in copies:
            copy.wait()

    return pl.pallas_call(
        kernel,
        in_specs=[pl.BlockSpec(memory_space=pltpu.SMEM)]
        + [pl.BlockSpec(memory_space=pltpu.VMEM)] * 9,
        out_specs=[pl.BlockSpec(memory_space=pltpu.HBM)] * 3,
        out_shape=[shape(ROWS, F, jnp.float32)] * 3,
        scratch_shapes=[pltpu.VMEM((ROWS, F), jnp.float32)] * 3
        + [pltpu.SemaphoreType.DMA((3, ROWS // STRIP))],
        cost_estimate=SMALL,
        compiler_params=VMEM,
        name="adam",
    )(frag_index, *grads, adam_m, adam_v, master, new_global)


def body(
    token_in, cotangent, weight, adam_m, adam_v, pseudo_grad, momentum, global_frag, frag_index
):
    tokens = token_in[0]
    up_own = cotangent[0]
    master = weight[0]

    send_x, send_far = pieces_of(tokens, up_own, [((1, 0, 0, TOK, 1),), ((1, 1, 0, TOK, 0),)])
    tok_x = swap_x(send_x)
    for_far = swap_core(send_far)
    tok_far = swap_x(for_far)
    weight_bf = after(master.astype(jnp.bfloat16), send_x)
    block_1 = shift_y(weight_bf, -1)
    block_3 = shift_y(weight_bf, 1)
    tok_own, send_core = pieces_of(
        after(tokens, send_x), up_own, [((0, 0, 0, TOK, 0),), ((0, 1, 0, TOK, 0),)]
    )
    tok_core = swap_core(send_core)
    up_x = tok_x[:, PIECE:]
    up_pair = swap_core(jnp.concatenate([up_own, up_x]))
    block_2a = shift_y(block_1[:HALF], -1)
    block_2b = shift_y(block_3[HALF:], 1)
    blocks = (weight_bf, block_1, block_3, block_2a, block_2b)

    total = replica_step(after(pseudo_grad[0].astype(jnp.bfloat16), tok_core, for_far), lambda i: i ^ 6)
    total = replica_step(total, lambda i: i ^ 1)
    up_ready, total = lax.optimization_barrier((up_own, total))
    toks = (tok_own, tok_x, tok_core, tok_far)
    g0, to_above, to_below, keep_above, keep_below = weight_grad(toks, (up_ready, up_x, up_pair))
    from_below, from_above = shift_y(to_above, 1), shift_y(to_below, -1)

    ig_own, ig_x, ig_core, ig_far = input_grad((after(up_ready, g0), up_x, up_pair), blocks)
    back_x = swap_x(ig_x)
    back_far = swap_core(ig_far)
    back_core = swap_core(ig_core)
    other_a = swap_x(split(back_far))

    val_own, val_x, val_pair = value_parts(toks, (after(weight_bf, g0), *blocks[1:]))
    val_back = swap_core(val_pair)
    other_b = swap_x(after(pack(back_far, val_back, val_x), other_a))
    total = replica_step(after(total, back_core), lambda i: i ^ 2)

    s1, s3 = relay(after(keep_above, back_x), keep_below, from_below, from_above)
    r1 = shift_y(s1, 1)
    r3 = shift_y(s3, -1)

    total = replica_step(after(total, s1), lambda i: i ^ 8)
    new_momentum, new_global = outer_update(momentum, global_frag, total / 16)

    block = assemble(
        None,
        (ig_own, back_core, back_x, other_a),
        ((0, 0, 0, TOK), (0, 1, 0, TOK), (1, 0, 0, TOK), (1, 1, 0, FIRST)),
    )
    new_weight, new_m, new_v = adam(
        frag_index, (g0, from_above, r1, from_below, r3), adam_m[0], adam_v[0], master, after(new_global, block)
    )
    block, values = assemble(
        block, (after(other_b, new_weight),), ((1, 1, FIRST, TOK - FIRST),), (val_own, val_back)
    )
    return (
        values[None],
        block[None],
        new_weight[None],
        new_m[None],
        new_v[None],
        new_global,
        new_momentum,
    )


def solution(mesh):
    in_specs = (
        P("replica", "fsdp", None),
        P("replica", "fsdp", None),
        P("replica", "fsdp", None),
        P("replica", "fsdp", None),
        P("replica", "fsdp", None),
        P("replica", "fsdp", None),
        P("fsdp", None),
        P("fsdp", None),
        P(),
    )
    out_specs = (
        P("replica", "fsdp", None),
        P("replica", "fsdp", None),
        P("replica", "fsdp", None),
        P("replica", "fsdp", None),
        P("replica", "fsdp", None),
        P("fsdp", None),
        P("fsdp", None),
    )
    return jax.shard_map(body, mesh=mesh, in_specs=in_specs, out_specs=out_specs, check_vma=False)
```

```python
import functools

import jax
import jax.numpy as jnp
from jax import lax
from jax.experimental import pallas as pl
from jax.experimental.pallas import tpu as pltpu
from jax.sharding import PartitionSpec as P

D = 8192
SCALE = D ** (-0.5)

beta_first = 0.9
beta_second = 0.95
epsilon = 1e-08
inner_rate = 0.01
decay_rate = 0.1
outer_rate = 0.7
outer_mom = 0.9
mix_share = 0.5

NY = 4
TOK = 128
ROWS = 512
F = 512
PIECE = NY * ROWS
HALF = ROWS // 2
FIRST = 96
LATER = 320
VMEM = pltpu.CompilerParams(vmem_limit_bytes=40 * 1024 * 1024)


def fsdp_permute(value, target):
    pairs = []
    for i in range(16):
        x, y, c = i // 8, (i // 2) % NY, i % 2
        x2, y2, c2 = target(x, y, c)
        pairs.append((i, ((x2 % 2) * NY + y2 % NY) * 2 + c2 % 2))
    return lax.ppermute(value, "fsdp", pairs)


def swap_x(value):
    return fsdp_permute(value, lambda x, y, c: (x + 1, y, c))


def swap_core(value):
    return fsdp_permute(value, lambda x, y, c: (x, y, c + 1))


def shift_y(value, step):
    return fsdp_permute(value, lambda x, y, c: (x, y + step, c))


def replica_step(total, partner):
    sent = total.astype(jnp.bfloat16)
    other = lax.ppermute(sent, "replica", [(i, partner(i)) for i in range(16)])
    return sent.astype(jnp.float32) + other.astype(jnp.float32)


def after(value, *others):
    return lax.optimization_barrier((value, *others))[0]


def outer_update(momentum, global_frag, average):
    mom_new = outer_mom * momentum + average
    glob_new = global_frag - outer_rate * (outer_mom * mom_new + average)
    return (mom_new, glob_new)


def shape(rows, cols, dtype=jnp.bfloat16):
    return jax.ShapeDtypeStruct((rows, cols), dtype)


SMALL = pl.CostEstimate(flops=1, bytes_accessed=1, transcendentals=0)


def here():
    device = lax.axis_index("fsdp")
    return device // (2 * NY), lax.rem(device // 2, NY), lax.rem(device, 2)


def column(x, y, c):
    return pl.ds(pl.multiple_of(((x * NY + y) * 2 + c) * ROWS, ROWS), ROWS)


def pieces_of(tokens, up, wanted):
    groups = [(i, g) for i, stack in enumerate(wanted) for g in stack]

    def kernel(source, up_ref, *refs):
        targets, sems = refs[:-1], refs[-1]
        x, _, c = here()
        copies, filled = [], [0] * len(wanted)
        for n, (i, (dx, dc, start, size, with_up)) in enumerate(groups):
            rows, into = pl.ds(start, size), pl.ds(filled[i], size)
            filled[i] += size
            moves = [
                (
                    source.at[rows, column(1 - x if dx else x, k, 1 - c if dc else c)],
                    targets[i].at[into, pl.ds(k * ROWS, ROWS)],
                )
                for k in range(NY)
            ]
            if with_up:
                moves.append((up_ref.at[rows], targets[i].at[into, pl.ds(PIECE, F)]))
            for k, (here_from, here_to) in enumerate(moves):
                copies.append(pltpu.make_async_copy(here_from, here_to, sems.at[n, k]))
        for copy in copies:
            copy.start()
        for copy in copies:
            copy.wait()

    return pl.pallas_call(
        kernel,
        in_specs=[pl.BlockSpec(memory_space=pltpu.VMEM), pl.BlockSpec(memory_space=pltpu.HBM)],
        out_specs=[pl.BlockSpec(memory_space=pltpu.VMEM)] * len(wanted),
        out_shape=[
            shape(sum(g[3] for g in stack), PIECE + F * stack[0][4]) for stack in wanted
        ],
        scratch_shapes=[pltpu.SemaphoreType.DMA((len(groups), NY + 1))],
        cost_estimate=SMALL,
        compiler_params=VMEM,
        name="pieces",
    )(tokens, up)


def places(blocks):
    y = here()[1]
    for (step, start), block in zip(((0, 0), (1, 0), (3, 0), (2, 0), (2, HALF)), blocks, strict=True):
        at = pl.multiple_of(lax.rem(y + step, NY) * ROWS + start, HALF)
        yield pl.ds(at, block.shape[0]), block


def input_grad(ups, blocks):
    def kernel(u0, u1, u2, *refs):
        up = jnp.concatenate([u0[...], u1[...], u2[...]], axis=0)
        for at, block in places(refs[:5]):
            grad = lax.dot_general(
                up, block[...], (((1,), (1,)), ((), ())), preferred_element_type=jnp.float32
            )
            grad = (grad * SCALE).astype(jnp.bfloat16)
            for k, out in enumerate(refs[5:]):
                out[:, at] = grad[k * TOK : (k + 1) * TOK]

    return pl.pallas_call(
        kernel,
        in_specs=[pl.BlockSpec(memory_space=pltpu.VMEM)] * 8,
        out_specs=[pl.BlockSpec(memory_space=pltpu.VMEM)] * 4,
        out_shape=[shape(TOK, PIECE)] * 4,
        cost_estimate=SMALL,
        compiler_params=VMEM,
        name="input_grad",
    )(*ups, *blocks)


def value_parts(toks, blocks):
    def kernel(t0, t1, t2, t3, *refs):
        own, far, pair = refs[5:]
        total = jnp.zeros((4 * TOK, F), jnp.float32)
        for at, block in places(refs[:5]):
            tok = jnp.concatenate([t0[:, at], t1[:, at], t2[:, at], t3[:, at]], axis=0)
            total += jnp.dot(tok, block[...], preferred_element_type=jnp.float32)
        own[...] = total[:TOK]
        far[...] = total[TOK : 2 * TOK]
        pair[...] = total[2 * TOK :].astype(jnp.bfloat16)

    return pl.pallas_call(
        kernel,
        in_specs=[pl.BlockSpec(memory_space=pltpu.VMEM)] * 9,
        out_specs=[pl.BlockSpec(memory_space=pltpu.VMEM)] * 3,
        out_shape=[shape(TOK, F, jnp.float32)] * 2 + [shape(2 * TOK, F)],
        cost_estimate=SMALL,
        compiler_params=VMEM,
        name="values",
    )(*toks, *blocks)


def split(passed):
    def kernel(passed, out):
        out[...] = passed[:FIRST]

    return pl.pallas_call(
        kernel,
        in_specs=[pl.BlockSpec(memory_space=pltpu.VMEM)],
        out_specs=pl.BlockSpec(memory_space=pltpu.VMEM),
        out_shape=shape(FIRST, PIECE),
        cost_estimate=SMALL,
        compiler_params=VMEM,
        name="split",
    )(passed)


def pack(passed, val_back, val_x):
    rest = TOK - FIRST

    def kernel(passed, val_back, val_x, out):
        out[:rest] = passed[FIRST:]
        total = val_x[...] + val_back[TOK:].astype(jnp.float32)
        for k in range(NY):
            rows = slice(k * rest, (k + 1) * rest)
            out[rest:, k * F : (k + 1) * F] = total[rows].astype(jnp.bfloat16)

    return pl.pallas_call(
        kernel,
        in_specs=[pl.BlockSpec(memory_space=pltpu.VMEM)] * 3,
        out_specs=pl.BlockSpec(memory_space=pltpu.VMEM),
        out_shape=shape(2 * rest, PIECE),
        cost_estimate=SMALL,
        compiler_params=VMEM,
        name="pack",
    )(passed, val_back, val_x)


def weight_grad(toks, ups):
    def kernel(t0, t1, t2, t3, u0, u1, u2, own, to_above, to_below, keep_above, keep_below):
        up = jnp.concatenate([u0[...], u1[...], u2[...]], axis=0)
        y = here()[1]

        def block(step):
            at = pl.ds(pl.multiple_of(lax.rem(y + step, NY) * ROWS, ROWS), ROWS)
            tok = jnp.concatenate([t0[:, at], t1[:, at], t2[:, at], t3[:, at]], axis=0)
            return SCALE * lax.dot_general(
                tok, up, (((0,), (0,)), ((), ())), preferred_element_type=jnp.float32
            )

        grad = block(2)
        to_above[:HALF] = grad[:HALF].astype(jnp.bfloat16)
        to_below[:HALF] = grad[HALF:].astype(jnp.bfloat16)
        grad = block(1)
        keep_above[...] = grad[:LATER]
        to_above[HALF:] = grad[LATER:].astype(jnp.bfloat16)
        grad = block(3)
        to_below[HALF:] = grad[: ROWS - LATER].astype(jnp.bfloat16)
        keep_below[...] = grad[ROWS - LATER :]
        own[...] = block(0)

    return pl.pallas_call(
        kernel,
        in_specs=[pl.BlockSpec(memory_space=pltpu.VMEM)] * 7,
        out_specs=[pl.BlockSpec(memory_space=pltpu.VMEM)] * 5,
        out_shape=[shape(ROWS, F, jnp.float32)]
        + [shape(HALF + ROWS - LATER, F)] * 2
        + [shape(LATER, F, jnp.float32)] * 2,
        cost_estimate=SMALL,
        compiler_params=VMEM,
        name="weight_grad",
    )(*toks, *ups)


def relay(keep_above, keep_below, from_below, from_above):
    def kernel(keep_above, keep_below, from_below, from_above, to_above, to_below):
        more = LATER - HALF
        came = from_below[:HALF].astype(jnp.float32)
        to_above[:HALF] = (keep_above[:HALF] + came).astype(jnp.bfloat16)
        to_above[HALF:] = keep_above[HALF:].astype(jnp.bfloat16)
        came = from_above[:HALF].astype(jnp.float32)
        to_below[:more] = keep_below[:more].astype(jnp.bfloat16)
        to_below[more:] = (keep_below[more:] + came).astype(jnp.bfloat16)

    return pl.pallas_call(
        kernel,
        in_specs=[pl.BlockSpec(memory_space=pltpu.VMEM)] * 4,
        out_specs=[pl.BlockSpec(memory_space=pltpu.VMEM)] * 2,
        out_shape=[shape(LATER, F)] * 2,
        cost_estimate=SMALL,
        compiler_params=VMEM,
        name="relay",
    )(keep_above, keep_below, from_below, from_above)


def assemble(block, parts, wanted, vals=()):
    n = len(wanted)

    def kernel(*refs):
        *_, target, sems = refs if not vals else (refs[-4], refs[-1])
        x, _, c = here()
        copies = []
        for i, (dx, dc, start, size) in enumerate(wanted):
            for k in range(NY):
                place = column(1 - x if dx else x, k, 1 - c if dc else c)
                copies.append(
                    pltpu.make_async_copy(
                        refs[i].at[pl.ds(0, size), pl.ds(k * ROWS, ROWS)],
                        target.at[pl.ds(start, size), place],
                        sems.at[i * NY + k],
                    )
                )
        for copy in copies:
            copy.start()
        if vals:
            own, pair = refs[n : n + 2]
            rest = TOK - FIRST
            total = own[...] + pair[:TOK].astype(jnp.float32)
            for k in range(NY):
                rows = slice(k * rest, (k + 1) * rest)
                came = refs[n - 1][rest:, k * F : (k + 1) * F].astype(jnp.float32)
                refs[-2][rows] = ((total[rows] + came) * SCALE).astype(jnp.bfloat16)
            copies.append(pltpu.make_async_copy(refs[-2], refs[-3], sems.at[NY * n]))
            copies[-1].start()
        for copy in copies:
            copy.wait()

    args = [*parts, *vals]
    ins = [pl.BlockSpec(memory_space=pltpu.VMEM)] * len(args)
    outs, shapes, alias = [pl.BlockSpec(memory_space=pltpu.HBM)], [shape(TOK, D)], {}
    if vals:
        outs.append(pl.BlockSpec(memory_space=pltpu.HBM))
        shapes.append(shape(TOK, F))
    if block is not None:
        alias = {len(args): 0}
        ins.append(pl.BlockSpec(memory_space=pltpu.HBM))
        args.append(block)
    return pl.pallas_call(
        kernel,
        in_specs=ins,
        out_specs=outs if vals else outs[0],
        out_shape=shapes if vals else shapes[0],
        scratch_shapes=[pltpu.VMEM((TOK, F), jnp.bfloat16)] * bool(vals)
        + [pltpu.SemaphoreType.DMA((NY * n + 1,))],
        input_output_aliases=alias,
        cost_estimate=SMALL,
        compiler_params=VMEM,
        name="assemble",
    )(*args)


STRIP = 64


def adam(frag_index, grads, adam_m, adam_v, master, new_global):
    def kernel(frag, g0, from_above, r1, from_below, r3, m, v, w, glob, hbm_w, hbm_m, hbm_v, new_w, new_m, new_v, sems):
        at = pl.ds(pl.multiple_of(frag[0] * 128, 128), 128)
        copies = []
        for k in range(ROWS // STRIP):
            rows = pl.ds(k * STRIP, STRIP)
            top = k * STRIP
            if top < LATER:
                grad = g0[rows, :] + r1[rows, :].astype(jnp.float32)
            else:
                came = from_below[pl.ds(HALF + top - LATER, STRIP), :]
                grad = g0[rows, :] + came.astype(jnp.float32)
            if top < ROWS - LATER:
                grad = grad + from_above[pl.ds(HALF + top, STRIP), :].astype(jnp.float32)
            else:
                came = r3[pl.ds(top - (ROWS - LATER), STRIP), :]
                grad = grad + came.astype(jnp.float32)
            mom = beta_first * m[rows, :] + (1.0 - beta_first) * grad
            var = beta_second * v[rows, :] + (1.0 - beta_second) * grad * grad
            new_m[rows, :] = mom
            new_v[rows, :] = var
            old = w[rows, :]
            new_w[rows, :] = old - inner_rate * (
                mom / (jnp.sqrt(var) + epsilon) + decay_rate * old
            )
            new_w[rows, at] = mix_share * new_w[rows, at] + (1.0 - mix_share) * glob[rows, :]
            for i, (source, target) in enumerate(
                ((new_w, hbm_w), (new_m, hbm_m), (new_v, hbm_v))
            ):
                copy = pltpu.make_async_copy(source.at[rows], target.at[rows], sems.at[i, k])
                copy.start()
                copies.append(copy)
        for copy in copies:
            copy.wait()

    return pl.pallas_call(
        kernel,
        in_specs=[pl.BlockSpec(memory_space=pltpu.SMEM)]
        + [pl.BlockSpec(memory_space=pltpu.VMEM)] * 9,
        out_specs=[pl.BlockSpec(memory_space=pltpu.HBM)] * 3,
        out_shape=[shape(ROWS, F, jnp.float32)] * 3,
        scratch_shapes=[pltpu.VMEM((ROWS, F), jnp.float32)] * 3
        + [pltpu.SemaphoreType.DMA((3, ROWS // STRIP))],
        cost_estimate=SMALL,
        compiler_params=VMEM,
        name="adam",
    )(frag_index, *grads, adam_m, adam_v, master, new_global)


def body(
    token_in, cotangent, weight, adam_m, adam_v, pseudo_grad, momentum, global_frag, frag_index
):
    tokens = token_in[0]
    up_own = cotangent[0]
    master = weight[0]

    send_x, send_far = pieces_of(tokens, up_own, [((1, 0, 0, TOK, 1),), ((1, 1, 0, TOK, 0),)])
    tok_x = swap_x(send_x)
    for_far = swap_core(send_far)
    tok_far = swap_x(for_far)
    weight_bf = after(master.astype(jnp.bfloat16), send_x)
    block_1 = shift_y(weight_bf, -1)
    block_3 = shift_y(weight_bf, 1)
    tok_own, send_core = pieces_of(
        after(tokens, send_x), up_own, [((0, 0, 0, TOK, 0),), ((0, 1, 0, TOK, 0),)]
    )
    tok_core = swap_core(send_core)
    up_x = tok_x[:, PIECE:]
    up_pair = swap_core(jnp.concatenate([up_own, up_x]))
    block_2a = shift_y(block_1[:HALF], -1)
    block_2b = shift_y(block_3[HALF:], 1)
    blocks = (weight_bf, block_1, block_3, block_2a, block_2b)

    total = replica_step(after(pseudo_grad[0].astype(jnp.bfloat16), tok_core, for_far), lambda i: i ^ 6)
    total = replica_step(total, lambda i: i ^ 1)
    up_ready, total = lax.optimization_barrier((up_own, total))
    toks = (tok_own, tok_x, tok_core, tok_far)
    g0, to_above, to_below, keep_above, keep_below = weight_grad(toks, (up_ready, up_x, up_pair))
    from_below, from_above = shift_y(to_above, 1), shift_y(to_below, -1)

    ig_own, ig_x, ig_core, ig_far = input_grad((after(up_ready, g0), up_x, up_pair), blocks)
    back_x = swap_x(ig_x)
    back_far = swap_core(ig_far)
    back_core = swap_core(ig_core)
    other_a = swap_x(split(back_far))

    val_own, val_x, val_pair = value_parts(toks, (after(weight_bf, g0), *blocks[1:]))
    val_back = swap_core(val_pair)
    other_b = swap_x(pack(back_far, val_back, val_x))
    total = replica_step(after(total, back_core), lambda i: i ^ 2)

    s1, s3 = relay(after(keep_above, back_x), keep_below, from_below, from_above)
    r1 = shift_y(s1, 1)
    r3 = shift_y(s3, -1)

    total = replica_step(after(total, s1), lambda i: i ^ 8)
    new_momentum, new_global = outer_update(momentum, global_frag, total / 16)

    block = assemble(
        None,
        (ig_own, back_core, back_x, other_a),
        ((0, 0, 0, TOK), (0, 1, 0, TOK), (1, 0, 0, TOK), (1, 1, 0, FIRST)),
    )
    new_weight, new_m, new_v = adam(
        frag_index, (g0, from_above, r1, from_below, r3), adam_m[0], adam_v[0], master, after(new_global, block)
    )
    block, values = assemble(
        block, (after(other_b, new_weight),), ((1, 1, FIRST, TOK - FIRST),), (val_own, val_back)
    )
    return (
        values[None],
        block[None],
        new_weight[None],
        new_m[None],
        new_v[None],
        new_global,
        new_momentum,
    )


def solution(mesh):
    in_specs = (
        P("replica", "fsdp", None),
        P("replica", "fsdp", None),
        P("replica", "fsdp", None),
        P("replica", "fsdp", None),
        P("replica", "fsdp", None),
        P("replica", "fsdp", None),
        P("fsdp", None),
        P("fsdp", None),
        P(),
    )
    out_specs = (
        P("replica", "fsdp", None),
        P("replica", "fsdp", None),
        P("replica", "fsdp", None),
        P("replica", "fsdp", None),
        P("replica", "fsdp", None),
        P("fsdp", None),
        P("fsdp", None),
    )
    return jax.shard_map(body, mesh=mesh, in_specs=in_specs, out_specs=out_specs, check_vma=False)
```

```python
import functools

import jax
import jax.numpy as jnp
from jax import lax
from jax.experimental import pallas as pl
from jax.experimental.pallas import tpu as pltpu
from jax.sharding import PartitionSpec as P

D = 8192
SCALE = D ** (-0.5)

beta_first = 0.9
beta_second = 0.95
epsilon = 1e-08
inner_rate = 0.01
decay_rate = 0.1
outer_rate = 0.7
outer_mom = 0.9
mix_share = 0.5

NY = 4
TOK = 128
ROWS = 512
F = 512
PIECE = NY * ROWS
HALF = ROWS // 2
FIRST = 96
LATER = 320
VMEM = pltpu.CompilerParams(vmem_limit_bytes=40 * 1024 * 1024)


def fsdp_permute(value, target):
    pairs = []
    for i in range(16):
        x, y, c = i // 8, (i // 2) % NY, i % 2
        x2, y2, c2 = target(x, y, c)
        pairs.append((i, ((x2 % 2) * NY + y2 % NY) * 2 + c2 % 2))
    return lax.ppermute(value, "fsdp", pairs)


def swap_x(value):
    return fsdp_permute(value, lambda x, y, c: (x + 1, y, c))


def swap_core(value):
    return fsdp_permute(value, lambda x, y, c: (x, y, c + 1))


def shift_y(value, step):
    return fsdp_permute(value, lambda x, y, c: (x, y + step, c))


def replica_step(total, partner):
    sent = total.astype(jnp.bfloat16)
    other = lax.ppermute(sent, "replica", [(i, partner(i)) for i in range(16)])
    return sent.astype(jnp.float32) + other.astype(jnp.float32)


def after(value, *others):
    return lax.optimization_barrier((value, *others))[0]


def outer_update(momentum, global_frag, average):
    mom_new = outer_mom * momentum + average
    glob_new = global_frag - outer_rate * (outer_mom * mom_new + average)
    return (mom_new, glob_new)


def shape(rows, cols, dtype=jnp.bfloat16):
    return jax.ShapeDtypeStruct((rows, cols), dtype)


SMALL = pl.CostEstimate(flops=1, bytes_accessed=1, transcendentals=0)


def here():
    device = lax.axis_index("fsdp")
    return device // (2 * NY), lax.rem(device // 2, NY), lax.rem(device, 2)


def column(x, y, c):
    return pl.ds(pl.multiple_of(((x * NY + y) * 2 + c) * ROWS, ROWS), ROWS)


def pieces_of(tokens, up, wanted):
    groups = [(i, g) for i, stack in enumerate(wanted) for g in stack]

    def kernel(source, up_ref, *refs):
        targets, sems = refs[:-1], refs[-1]
        x, _, c = here()
        copies, filled = [], [0] * len(wanted)
        for n, (i, (dx, dc, start, size, with_up)) in enumerate(groups):
            rows, into = pl.ds(start, size), pl.ds(filled[i], size)
            filled[i] += size
            moves = [
                (
                    source.at[rows, column(1 - x if dx else x, k, 1 - c if dc else c)],
                    targets[i].at[into, pl.ds(k * ROWS, ROWS)],
                )
                for k in range(NY)
            ]
            if with_up:
                moves.append((up_ref.at[rows], targets[i].at[into, pl.ds(PIECE, F)]))
            for k, (here_from, here_to) in enumerate(moves):
                copies.append(pltpu.make_async_copy(here_from, here_to, sems.at[n, k]))
        for copy in copies:
            copy.start()
        for copy in copies:
            copy.wait()

    return pl.pallas_call(
        kernel,
        in_specs=[pl.BlockSpec(memory_space=pltpu.VMEM), pl.BlockSpec(memory_space=pltpu.HBM)],
        out_specs=[pl.BlockSpec(memory_space=pltpu.VMEM)] * len(wanted),
        out_shape=[
            shape(sum(g[3] for g in stack), PIECE + F * stack[0][4]) for stack in wanted
        ],
        scratch_shapes=[pltpu.SemaphoreType.DMA((len(groups), NY + 1))],
        cost_estimate=SMALL,
        compiler_params=VMEM,
        name="pieces",
    )(tokens, up)


def places(blocks):
    y = here()[1]
    for (step, start), block in zip(((0, 0), (1, 0), (3, 0), (2, 0), (2, HALF)), blocks, strict=True):
        at = pl.multiple_of(lax.rem(y + step, NY) * ROWS + start, HALF)
        yield pl.ds(at, block.shape[0]), block


def input_grad(ups, blocks):
    def kernel(u0, u1, u2, *refs):
        up = jnp.concatenate([u0[...], u1[...], u2[...]], axis=0)
        for at, block in places(refs[:5]):
            grad = lax.dot_general(
                up, block[...], (((1,), (1,)), ((), ())), preferred_element_type=jnp.float32
            )
            grad = (grad * SCALE).astype(jnp.bfloat16)
            for k, out in enumerate(refs[5:]):
                out[:, at] = grad[k * TOK : (k + 1) * TOK]

    return pl.pallas_call(
        kernel,
        in_specs=[pl.BlockSpec(memory_space=pltpu.VMEM)] * 8,
        out_specs=[pl.BlockSpec(memory_space=pltpu.VMEM)] * 4,
        out_shape=[shape(TOK, PIECE)] * 4,
        cost_estimate=SMALL,
        compiler_params=VMEM,
        name="input_grad",
    )(*ups, *blocks)


def value_parts(toks, blocks):
    def kernel(t0, t1, t2, t3, *refs):
        own, far, pair = refs[5:]
        total = jnp.zeros((4 * TOK, F), jnp.float32)
        for at, block in places(refs[:5]):
            tok = jnp.concatenate([t0[:, at], t1[:, at], t2[:, at], t3[:, at]], axis=0)
            total += jnp.dot(tok, block[...], preferred_element_type=jnp.float32)
        own[...] = total[:TOK]
        far[...] = total[TOK : 2 * TOK]
        pair[...] = total[2 * TOK :].astype(jnp.bfloat16)

    return pl.pallas_call(
        kernel,
        in_specs=[pl.BlockSpec(memory_space=pltpu.VMEM)] * 9,
        out_specs=[pl.BlockSpec(memory_space=pltpu.VMEM)] * 3,
        out_shape=[shape(TOK, F, jnp.float32)] * 2 + [shape(2 * TOK, F)],
        cost_estimate=SMALL,
        compiler_params=VMEM,
        name="values",
    )(*toks, *blocks)


def split(passed):
    def kernel(passed, out):
        out[...] = passed[:FIRST]

    return pl.pallas_call(
        kernel,
        in_specs=[pl.BlockSpec(memory_space=pltpu.VMEM)],
        out_specs=pl.BlockSpec(memory_space=pltpu.VMEM),
        out_shape=shape(FIRST, PIECE),
        cost_estimate=SMALL,
        compiler_params=VMEM,
        name="split",
    )(passed)


def pack(passed, val_back, val_x):
    rest = TOK - FIRST

    def kernel(passed, val_back, val_x, out):
        out[:rest] = passed[FIRST:]
        total = val_x[...] + val_back[TOK:].astype(jnp.float32)
        for k in range(NY):
            rows = slice(k * rest, (k + 1) * rest)
            out[rest:, k * F : (k + 1) * F] = total[rows].astype(jnp.bfloat16)

    return pl.pallas_call(
        kernel,
        in_specs=[pl.BlockSpec(memory_space=pltpu.VMEM)] * 3,
        out_specs=pl.BlockSpec(memory_space=pltpu.VMEM),
        out_shape=shape(2 * rest, PIECE),
        cost_estimate=SMALL,
        compiler_params=VMEM,
        name="pack",
    )(passed, val_back, val_x)


def token_sum(toks, ups):
    return lax.dot_general(
        jnp.concatenate(toks, axis=0),
        jnp.concatenate(ups, axis=0),
        (((0,), (0,)), ((), ())),
        preferred_element_type=jnp.float32,
    )


def weight_grad_before(toks, ups):
    def kernel(t0, t1, t2, u0, u1, u2, out):
        y = here()[1]
        for step in range(NY):
            at = pl.ds(pl.multiple_of(lax.rem(y + step, NY) * ROWS, ROWS), ROWS)
            out[step] = SCALE * token_sum(
                [t0[:, at], t1[:, at], t2[:, at]], [u0[...], u1[...], u2[:TOK]]
            )

    return pl.pallas_call(
        kernel,
        in_specs=[pl.BlockSpec(memory_space=pltpu.VMEM)] * 6,
        out_specs=pl.BlockSpec(memory_space=pltpu.VMEM),
        out_shape=jax.ShapeDtypeStruct((NY, ROWS, F), jnp.float32),
        cost_estimate=SMALL,
        compiler_params=VMEM,
        name="weight_grad_before",
    )(*toks, *ups)


def weight_grad(tok_far, up_pair, before):
    def kernel(t3, u2, before, own, to_above, to_below, keep_above, keep_below):
        y = here()[1]

        def block(step):
            at = pl.ds(pl.multiple_of(lax.rem(y + step, NY) * ROWS, ROWS), ROWS)
            return before[step] + SCALE * token_sum([t3[:, at]], [u2[TOK:]])

        grad = block(2)
        to_above[:HALF] = grad[:HALF].astype(jnp.bfloat16)
        to_below[:HALF] = grad[HALF:].astype(jnp.bfloat16)
        grad = block(1)
        keep_above[...] = grad[:LATER]
        to_above[HALF:] = grad[LATER:].astype(jnp.bfloat16)
        grad = block(3)
        to_below[HALF:] = grad[: ROWS - LATER].astype(jnp.bfloat16)
        keep_below[...] = grad[ROWS - LATER :]
        own[...] = block(0)

    return pl.pallas_call(
        kernel,
        in_specs=[pl.BlockSpec(memory_space=pltpu.VMEM)] * 3,
        out_specs=[pl.BlockSpec(memory_space=pltpu.VMEM)] * 5,
        out_shape=[shape(ROWS, F, jnp.float32)]
        + [shape(HALF + ROWS - LATER, F)] * 2
        + [shape(LATER, F, jnp.float32)] * 2,
        cost_estimate=SMALL,
        compiler_params=VMEM,
        name="weight_grad",
    )(tok_far, up_pair, before)


def relay(keep_above, keep_below, from_below, from_above):
    def kernel(keep_above, keep_below, from_below, from_above, to_above, to_below):
        more = LATER - HALF
        came = from_below[:HALF].astype(jnp.float32)
        to_above[:HALF] = (keep_above[:HALF] + came).astype(jnp.bfloat16)
        to_above[HALF:] = keep_above[HALF:].astype(jnp.bfloat16)
        came = from_above[:HALF].astype(jnp.float32)
        to_below[:more] = keep_below[:more].astype(jnp.bfloat16)
        to_below[more:] = (keep_below[more:] + came).astype(jnp.bfloat16)

    return pl.pallas_call(
        kernel,
        in_specs=[pl.BlockSpec(memory_space=pltpu.VMEM)] * 4,
        out_specs=[pl.BlockSpec(memory_space=pltpu.VMEM)] * 2,
        out_shape=[shape(LATER, F)] * 2,
        cost_estimate=SMALL,
        compiler_params=VMEM,
        name="relay",
    )(keep_above, keep_below, from_below, from_above)


def assemble(block, parts, wanted, vals=()):
    n = len(wanted)

    def kernel(*refs):
        *_, target, sems = refs if not vals else (refs[-4], refs[-1])
        x, _, c = here()
        copies = []
        for i, (dx, dc, start, size) in enumerate(wanted):
            for k in range(NY):
                place = column(1 - x if dx else x, k, 1 - c if dc else c)
                copies.append(
                    pltpu.make_async_copy(
                        refs[i].at[pl.ds(0, size), pl.ds(k * ROWS, ROWS)],
                        target.at[pl.ds(start, size), place],
                        sems.at[i * NY + k],
                    )
                )
        for copy in copies:
            copy.start()
        if vals:
            own, pair = refs[n : n + 2]
            rest = TOK - FIRST
            total = own[...] + pair[:TOK].astype(jnp.float32)
            for k in range(NY):
                rows = slice(k * rest, (k + 1) * rest)
                came = refs[n - 1][rest:, k * F : (k + 1) * F].astype(jnp.float32)
                refs[-2][rows] = ((total[rows] + came) * SCALE).astype(jnp.bfloat16)
            copies.append(pltpu.make_async_copy(refs[-2], refs[-3], sems.at[NY * n]))
            copies[-1].start()
        for copy in copies:
            copy.wait()

    args = [*parts, *vals]
    ins = [pl.BlockSpec(memory_space=pltpu.VMEM)] * len(args)
    outs, shapes, alias = [pl.BlockSpec(memory_space=pltpu.HBM)], [shape(TOK, D)], {}
    if vals:
        outs.append(pl.BlockSpec(memory_space=pltpu.HBM))
        shapes.append(shape(TOK, F))
    if block is not None:
        alias = {len(args): 0}
        ins.append(pl.BlockSpec(memory_space=pltpu.HBM))
        args.append(block)
    return pl.pallas_call(
        kernel,
        in_specs=ins,
        out_specs=outs if vals else outs[0],
        out_shape=shapes if vals else shapes[0],
        scratch_shapes=[pltpu.VMEM((TOK, F), jnp.bfloat16)] * bool(vals)
        + [pltpu.SemaphoreType.DMA((NY * n + 1,))],
        input_output_aliases=alias,
        cost_estimate=SMALL,
        compiler_params=VMEM,
        name="assemble",
    )(*args)


STRIP = 64


def adam(frag_index, grads, adam_m, adam_v, master, new_global):
    def kernel(frag, g0, from_above, r1, from_below, r3, m, v, w, glob, hbm_w, hbm_m, hbm_v, new_w, new_m, new_v, sems):
        at = pl.ds(pl.multiple_of(frag[0] * 128, 128), 128)
        copies = []
        for k in range(ROWS // STRIP):
            rows = pl.ds(k * STRIP, STRIP)
            top = k * STRIP
            if top < LATER:
                grad = g0[rows, :] + r1[rows, :].astype(jnp.float32)
            else:
                came = from_below[pl.ds(HALF + top - LATER, STRIP), :]
                grad = g0[rows, :] + came.astype(jnp.float32)
            if top < ROWS - LATER:
                grad = grad + from_above[pl.ds(HALF + top, STRIP), :].astype(jnp.float32)
            else:
                came = r3[pl.ds(top - (ROWS - LATER), STRIP), :]
                grad = grad + came.astype(jnp.float32)
            mom = beta_first * m[rows, :] + (1.0 - beta_first) * grad
            var = beta_second * v[rows, :] + (1.0 - beta_second) * grad * grad
            new_m[rows, :] = mom
            new_v[rows, :] = var
            old = w[rows, :]
            new_w[rows, :] = old - inner_rate * (
                mom / (jnp.sqrt(var) + epsilon) + decay_rate * old
            )
            new_w[rows, at] = mix_share * new_w[rows, at] + (1.0 - mix_share) * glob[rows, :]
            for i, (source, target) in enumerate(
                ((new_w, hbm_w), (new_m, hbm_m), (new_v, hbm_v))
            ):
                copy = pltpu.make_async_copy(source.at[rows], target.at[rows], sems.at[i, k])
                copy.start()
                copies.append(copy)
        for copy in copies:
            copy.wait()

    return pl.pallas_call(
        kernel,
        in_specs=[pl.BlockSpec(memory_space=pltpu.SMEM)]
        + [pl.BlockSpec(memory_space=pltpu.VMEM)] * 9,
        out_specs=[pl.BlockSpec(memory_space=pltpu.HBM)] * 3,
        out_shape=[shape(ROWS, F, jnp.float32)] * 3,
        scratch_shapes=[pltpu.VMEM((ROWS, F), jnp.float32)] * 3
        + [pltpu.SemaphoreType.DMA((3, ROWS // STRIP))],
        cost_estimate=SMALL,
        compiler_params=VMEM,
        name="adam",
    )(frag_index, *grads, adam_m, adam_v, master, new_global)


def body(
    token_in, cotangent, weight, adam_m, adam_v, pseudo_grad, momentum, global_frag, frag_index
):
    tokens = token_in[0]
    up_own = cotangent[0]
    master = weight[0]

    send_x, send_far = pieces_of(tokens, up_own, [((1, 0, 0, TOK, 1),), ((1, 1, 0, TOK, 0),)])
    tok_x = swap_x(send_x)
    for_far = swap_core(send_far)
    tok_far = swap_x(for_far)
    weight_bf = after(master.astype(jnp.bfloat16), send_x)
    block_1 = shift_y(weight_bf, -1)
    block_3 = shift_y(weight_bf, 1)
    tok_own, send_core = pieces_of(
        after(tokens, send_x), up_own, [((0, 0, 0, TOK, 0),), ((0, 1, 0, TOK, 0),)]
    )
    tok_core = swap_core(send_core)
    up_x = tok_x[:, PIECE:]
    up_pair = swap_core(jnp.concatenate([up_own, up_x]))
    block_2a = shift_y(block_1[:HALF], -1)
    block_2b = shift_y(block_3[HALF:], 1)
    blocks = (weight_bf, block_1, block_3, block_2a, block_2b)

    total = replica_step(after(pseudo_grad[0].astype(jnp.bfloat16), tok_core, for_far), lambda i: i ^ 6)
    total = replica_step(total, lambda i: i ^ 1)
    up_ready, total = lax.optimization_barrier((up_own, total))
    toks = (tok_own, tok_x, tok_core, tok_far)
    before = weight_grad_before((tok_own, tok_x, tok_core), (up_ready, up_x, up_pair))
    g0, to_above, to_below, keep_above, keep_below = weight_grad(tok_far, up_pair, before)
    from_below, from_above = shift_y(to_above, 1), shift_y(to_below, -1)

    ig_own, ig_x, ig_core, ig_far = input_grad((after(up_ready, g0), up_x, up_pair), blocks)
    back_x = swap_x(ig_x)
    back_far = swap_core(ig_far)
    back_core = swap_core(ig_core)
    other_a = swap_x(split(back_far))

    val_own, val_x, val_pair = value_parts(toks, (after(weight_bf, g0), *blocks[1:]))
    val_back = swap_core(val_pair)
    other_b = swap_x(after(pack(back_far, val_back, val_x), other_a))
    total = replica_step(after(total, back_core), lambda i: i ^ 2)

    s1, s3 = relay(after(keep_above, back_x), keep_below, from_below, from_above)
    r1 = shift_y(s1, 1)
    r3 = shift_y(s3, -1)

    total = replica_step(after(total, s1), lambda i: i ^ 8)
    new_momentum, new_global = outer_update(momentum, global_frag, total / 16)

    block = assemble(
        None,
        (ig_own, back_core, back_x, other_a),
        ((0, 0, 0, TOK), (0, 1, 0, TOK), (1, 0, 0, TOK), (1, 1, 0, FIRST)),
    )
    new_weight, new_m, new_v = adam(
        frag_index, (g0, from_above, r1, from_below, r3), adam_m[0], adam_v[0], master, after(new_global, block)
    )
    block, values = assemble(
        block, (after(other_b, new_weight),), ((1, 1, FIRST, TOK - FIRST),), (val_own, val_back)
    )
    return (
        values[None],
        block[None],
        new_weight[None],
        new_m[None],
        new_v[None],
        new_global,
        new_momentum,
    )


def solution(mesh):
    in_specs = (
        P("replica", "fsdp", None),
        P("replica", "fsdp", None),
        P("replica", "fsdp", None),
        P("replica", "fsdp", None),
        P("replica", "fsdp", None),
        P("replica", "fsdp", None),
        P("fsdp", None),
        P("fsdp", None),
        P(),
    )
    out_specs = (
        P("replica", "fsdp", None),
        P("replica", "fsdp", None),
        P("replica", "fsdp", None),
        P("replica", "fsdp", None),
        P("replica", "fsdp", None),
        P("fsdp", None),
        P("fsdp", None),
    )
    return jax.shard_map(body, mesh=mesh, in_specs=in_specs, out_specs=out_specs, check_vma=False)
```

```python
import functools

import jax
import jax.numpy as jnp
from jax import lax
from jax.experimental import pallas as pl
from jax.experimental.pallas import tpu as pltpu
from jax.sharding import PartitionSpec as P

D = 8192
SCALE = D ** (-0.5)

beta_first = 0.9
beta_second = 0.95
epsilon = 1e-08
inner_rate = 0.01
decay_rate = 0.1
outer_rate = 0.7
outer_mom = 0.9
mix_share = 0.5

NY = 4
TOK = 128
ROWS = 512
F = 512
PIECE = NY * ROWS
HALF = ROWS // 2
FIRST = 96
LATER = 320
VMEM = pltpu.CompilerParams(vmem_limit_bytes=40 * 1024 * 1024)


def fsdp_permute(value, target):
    pairs = []
    for i in range(16):
        x, y, c = i // 8, (i // 2) % NY, i % 2
        x2, y2, c2 = target(x, y, c)
        pairs.append((i, ((x2 % 2) * NY + y2 % NY) * 2 + c2 % 2))
    return lax.ppermute(value, "fsdp", pairs)


def swap_x(value):
    return fsdp_permute(value, lambda x, y, c: (x + 1, y, c))


def swap_core(value):
    return fsdp_permute(value, lambda x, y, c: (x, y, c + 1))


def shift_y(value, step):
    return fsdp_permute(value, lambda x, y, c: (x, y + step, c))


def replica_step(total, partner):
    sent = total.astype(jnp.bfloat16)
    other = lax.ppermute(sent, "replica", [(i, partner(i)) for i in range(16)])
    return sent.astype(jnp.float32) + other.astype(jnp.float32)


def after(value, *others):
    return lax.optimization_barrier((value, *others))[0]


def outer_update(momentum, global_frag, average):
    mom_new = outer_mom * momentum + average
    glob_new = global_frag - outer_rate * (outer_mom * mom_new + average)
    return (mom_new, glob_new)


def shape(rows, cols, dtype=jnp.bfloat16):
    return jax.ShapeDtypeStruct((rows, cols), dtype)


SMALL = pl.CostEstimate(flops=1, bytes_accessed=1, transcendentals=0)


def here():
    device = lax.axis_index("fsdp")
    return device // (2 * NY), lax.rem(device // 2, NY), lax.rem(device, 2)


def column(x, y, c):
    return pl.ds(pl.multiple_of(((x * NY + y) * 2 + c) * ROWS, ROWS), ROWS)


def pieces_of(tokens, up, wanted):
    groups = [(i, g) for i, stack in enumerate(wanted) for g in stack]

    def kernel(source, up_ref, *refs):
        targets, sems = refs[:-1], refs[-1]
        x, _, c = here()
        copies, filled = [], [0] * len(wanted)
        for n, (i, (dx, dc, start, size, with_up)) in enumerate(groups):
            rows, into = pl.ds(start, size), pl.ds(filled[i], size)
            filled[i] += size
            moves = [
                (
                    source.at[rows, column(1 - x if dx else x, k, 1 - c if dc else c)],
                    targets[i].at[into, pl.ds(k * ROWS, ROWS)],
                )
                for k in range(NY)
            ]
            if with_up:
                moves.append((up_ref.at[rows], targets[i].at[into, pl.ds(PIECE, F)]))
            for k, (here_from, here_to) in enumerate(moves):
                copies.append(pltpu.make_async_copy(here_from, here_to, sems.at[n, k]))
        for copy in copies:
            copy.start()
        for copy in copies:
            copy.wait()

    return pl.pallas_call(
        kernel,
        in_specs=[pl.BlockSpec(memory_space=pltpu.VMEM), pl.BlockSpec(memory_space=pltpu.HBM)],
        out_specs=[pl.BlockSpec(memory_space=pltpu.VMEM)] * len(wanted),
        out_shape=[
            shape(sum(g[3] for g in stack), PIECE + F * stack[0][4]) for stack in wanted
        ],
        scratch_shapes=[pltpu.SemaphoreType.DMA((len(groups), NY + 1))],
        cost_estimate=SMALL,
        compiler_params=VMEM,
        name="pieces",
    )(tokens, up)


PLACES = ((0, 0), (1, 0), (3, 0), (2, 0), (2, HALF))


def places(blocks, where=PLACES):
    y = here()[1]
    for (step, start), block in zip(where, blocks, strict=True):
        at = pl.multiple_of(lax.rem(y + step, NY) * ROWS + start, HALF)
        yield pl.ds(at, block.shape[0]), block


def input_grad(ups, blocks, where, before=()):
    n = len(blocks)

    def kernel(u0, u1, u2, *refs):
        up = jnp.concatenate([u0[...], u1[...], u2[...]], axis=0)
        for at, block in places(refs[:n], where):
            grad = lax.dot_general(
                up, block[...], (((1,), (1,)), ((), ())), preferred_element_type=jnp.float32
            )
            grad = (grad * SCALE).astype(jnp.bfloat16)
            for k, out in enumerate(refs[-4:]):
                out[:, at] = grad[k * TOK : (k + 1) * TOK]

    return pl.pallas_call(
        kernel,
        in_specs=[pl.BlockSpec(memory_space=pltpu.VMEM)] * (3 + n + len(before)),
        out_specs=[pl.BlockSpec(memory_space=pltpu.VMEM)] * 4,
        out_shape=[shape(TOK, PIECE)] * 4,
        input_output_aliases={3 + n + k: k for k in range(len(before))},
        cost_estimate=SMALL,
        compiler_params=VMEM,
        name="input_grad",
    )(*ups, *blocks, *before)


def value_parts(toks, blocks):
    def kernel(t0, t1, t2, t3, *refs):
        own, far, pair = refs[5:]
        total = jnp.zeros((4 * TOK, F), jnp.float32)
        for at, block in places(refs[:5]):
            tok = jnp.concatenate([t0[:, at], t1[:, at], t2[:, at], t3[:, at]], axis=0)
            total += jnp.dot(tok, block[...], preferred_element_type=jnp.float32)
        own[...] = total[:TOK]
        far[...] = total[TOK : 2 * TOK]
        pair[...] = total[2 * TOK :].astype(jnp.bfloat16)

    return pl.pallas_call(
        kernel,
        in_specs=[pl.BlockSpec(memory_space=pltpu.VMEM)] * 9,
        out_specs=[pl.BlockSpec(memory_space=pltpu.VMEM)] * 3,
        out_shape=[shape(TOK, F, jnp.float32)] * 2 + [shape(2 * TOK, F)],
        cost_estimate=SMALL,
        compiler_params=VMEM,
        name="values",
    )(*toks, *blocks)


def split(passed):
    def kernel(passed, out):
        out[...] = passed[:FIRST]

    return pl.pallas_call(
        kernel,
        in_specs=[pl.BlockSpec(memory_space=pltpu.VMEM)],
        out_specs=pl.BlockSpec(memory_space=pltpu.VMEM),
        out_shape=shape(FIRST, PIECE),
        cost_estimate=SMALL,
        compiler_params=VMEM,
        name="split",
    )(passed)


def pack(passed, val_back, val_x):
    rest = TOK - FIRST

    def kernel(passed, val_back, val_x, out):
        out[:rest] = passed[FIRST:]
        total = val_x[...] + val_back[TOK:].astype(jnp.float32)
        for k in range(NY):
            rows = slice(k * rest, (k + 1) * rest)
            out[rest:, k * F : (k + 1) * F] = total[rows].astype(jnp.bfloat16)

    return pl.pallas_call(
        kernel,
        in_specs=[pl.BlockSpec(memory_space=pltpu.VMEM)] * 3,
        out_specs=pl.BlockSpec(memory_space=pltpu.VMEM),
        out_shape=shape(2 * rest, PIECE),
        cost_estimate=SMALL,
        compiler_params=VMEM,
        name="pack",
    )(passed, val_back, val_x)


def weight_grad(toks, ups):
    def kernel(t0, t1, t2, t3, u0, u1, u2, own, to_above, to_below, keep_above, keep_below):
        up = jnp.concatenate([u0[...], u1[...], u2[...]], axis=0)
        y = here()[1]

        def block(step):
            at = pl.ds(pl.multiple_of(lax.rem(y + step, NY) * ROWS, ROWS), ROWS)
            tok = jnp.concatenate([t0[:, at], t1[:, at], t2[:, at], t3[:, at]], axis=0)
            return SCALE * lax.dot_general(
                tok, up, (((0,), (0,)), ((), ())), preferred_element_type=jnp.float32
            )

        grad = block(2)
        to_above[:HALF] = grad[:HALF].astype(jnp.bfloat16)
        to_below[:HALF] = grad[HALF:].astype(jnp.bfloat16)
        grad = block(1)
        keep_above[...] = grad[:LATER]
        to_above[HALF:] = grad[LATER:].astype(jnp.bfloat16)
        grad = block(3)
        to_below[HALF:] = grad[: ROWS - LATER].astype(jnp.bfloat16)
        keep_below[...] = grad[ROWS - LATER :]
        own[...] = block(0)

    return pl.pallas_call(
        kernel,
        in_specs=[pl.BlockSpec(memory_space=pltpu.VMEM)] * 7,
        out_specs=[pl.BlockSpec(memory_space=pltpu.VMEM)] * 5,
        out_shape=[shape(ROWS, F, jnp.float32)]
        + [shape(HALF + ROWS - LATER, F)] * 2
        + [shape(LATER, F, jnp.float32)] * 2,
        cost_estimate=SMALL,
        compiler_params=VMEM,
        name="weight_grad",
    )(*toks, *ups)


def relay(keep_above, keep_below, from_below, from_above):
    def kernel(keep_above, keep_below, from_below, from_above, to_above, to_below):
        more = LATER - HALF
        came = from_below[:HALF].astype(jnp.float32)
        to_above[:HALF] = (keep_above[:HALF] + came).astype(jnp.bfloat16)
        to_above[HALF:] = keep_above[HALF:].astype(jnp.bfloat16)
        came = from_above[:HALF].astype(jnp.float32)
        to_below[:more] = keep_below[:more].astype(jnp.bfloat16)
        to_below[more:] = (keep_below[more:] + came).astype(jnp.bfloat16)

    return pl.pallas_call(
        kernel,
        in_specs=[pl.BlockSpec(memory_space=pltpu.VMEM)] * 4,
        out_specs=[pl.BlockSpec(memory_space=pltpu.VMEM)] * 2,
        out_shape=[shape(LATER, F)] * 2,
        cost_estimate=SMALL,
        compiler_params=VMEM,
        name="relay",
    )(keep_above, keep_below, from_below, from_above)


def assemble(block, parts, wanted, vals=()):
    n = len(wanted)

    def kernel(*refs):
        *_, target, sems = refs if not vals else (refs[-4], refs[-1])
        x, _, c = here()
        copies = []
        for i, (dx, dc, start, size) in enumerate(wanted):
            for k in range(NY):
                place = column(1 - x if dx else x, k, 1 - c if dc else c)
                copies.append(
                    pltpu.make_async_copy(
                        refs[i].at[pl.ds(0, size), pl.ds(k * ROWS, ROWS)],
                        target.at[pl.ds(start, size), place],
                        sems.at[i * NY + k],
                    )
                )
        for copy in copies:
            copy.start()
        if vals:
            own, pair = refs[n : n + 2]
            rest = TOK - FIRST
            total = own[...] + pair[:TOK].astype(jnp.float32)
            for k in range(NY):
                rows = slice(k * rest, (k + 1) * rest)
                came = refs[n - 1][rest:, k * F : (k + 1) * F].astype(jnp.float32)
                refs[-2][rows] = ((total[rows] + came) * SCALE).astype(jnp.bfloat16)
            copies.append(pltpu.make_async_copy(refs[-2], refs[-3], sems.at[NY * n]))
            copies[-1].start()
        for copy in copies:
            copy.wait()

    args = [*parts, *vals]
    ins = [pl.BlockSpec(memory_space=pltpu.VMEM)] * len(args)
    outs, shapes, alias = [pl.BlockSpec(memory_space=pltpu.HBM)], [shape(TOK, D)], {}
    if vals:
        outs.append(pl.BlockSpec(memory_space=pltpu.HBM))
        shapes.append(shape(TOK, F))
    if block is not None:
        alias = {len(args): 0}
        ins.append(pl.BlockSpec(memory_space=pltpu.HBM))
        args.append(block)
    return pl.pallas_call(
        kernel,
        in_specs=ins,
        out_specs=outs if vals else outs[0],
        out_shape=shapes if vals else shapes[0],
        scratch_shapes=[pltpu.VMEM((TOK, F), jnp.bfloat16)] * bool(vals)
        + [pltpu.SemaphoreType.DMA((NY * n + 1,))],
        input_output_aliases=alias,
        cost_estimate=SMALL,
        compiler_params=VMEM,
        name="assemble",
    )(*args)


STRIP = 64


def adam(frag_index, grads, adam_m, adam_v, master, new_global):
    def kernel(frag, g0, from_above, r1, from_below, r3, m, v, w, glob, hbm_w, hbm_m, hbm_v, new_w, new_m, new_v, sems):
        at = pl.ds(pl.multiple_of(frag[0] * 128, 128), 128)
        copies = []
        for k in range(ROWS // STRIP):
            rows = pl.ds(k * STRIP, STRIP)
            top = k * STRIP
            if top < LATER:
                grad = g0[rows, :] + r1[rows, :].astype(jnp.float32)
            else:
                came = from_below[pl.ds(HALF + top - LATER, STRIP), :]
                grad = g0[rows, :] + came.astype(jnp.float32)
            if top < ROWS - LATER:
                grad = grad + from_above[pl.ds(HALF + top, STRIP), :].astype(jnp.float32)
            else:
                came = r3[pl.ds(top - (ROWS - LATER), STRIP), :]
                grad = grad + came.astype(jnp.float32)
            mom = beta_first * m[rows, :] + (1.0 - beta_first) * grad
            var = beta_second * v[rows, :] + (1.0 - beta_second) * grad * grad
            new_m[rows, :] = mom
            new_v[rows, :] = var
            old = w[rows, :]
            new_w[rows, :] = old - inner_rate * (
                mom / (jnp.sqrt(var) + epsilon) + decay_rate * old
            )
            new_w[rows, at] = mix_share * new_w[rows, at] + (1.0 - mix_share) * glob[rows, :]
            for i, (source, target) in enumerate(
                ((new_w, hbm_w), (new_m, hbm_m), (new_v, hbm_v))
            ):
                copy = pltpu.make_async_copy(source.at[rows], target.at[rows], sems.at[i, k])
                copy.start()
                copies.append(copy)
        for copy in copies:
            copy.wait()

    return pl.pallas_call(
        kernel,
        in_specs=[pl.BlockSpec(memory_space=pltpu.SMEM)]
        + [pl.BlockSpec(memory_space=pltpu.VMEM)] * 9,
        out_specs=[pl.BlockSpec(memory_space=pltpu.HBM)] * 3,
        out_shape=[shape(ROWS, F, jnp.float32)] * 3,
        scratch_shapes=[pltpu.VMEM((ROWS, F), jnp.float32)] * 3
        + [pltpu.SemaphoreType.DMA((3, ROWS // STRIP))],
        cost_estimate=SMALL,
        compiler_params=VMEM,
        name="adam",
    )(frag_index, *grads, adam_m, adam_v, master, new_global)


def body(
    token_in, cotangent, weight, adam_m, adam_v, pseudo_grad, momentum, global_frag, frag_index
):
    tokens = token_in[0]
    up_own = cotangent[0]
    master = weight[0]

    send_x, send_far = pieces_of(tokens, up_own, [((1, 0, 0, TOK, 1),), ((1, 1, 0, TOK, 0),)])
    tok_x = swap_x(send_x)
    for_far = swap_core(send_far)
    tok_far = swap_x(for_far)
    weight_bf = after(master.astype(jnp.bfloat16), send_x)
    block_1 = shift_y(weight_bf, -1)
    block_3 = shift_y(weight_bf, 1)
    tok_own, send_core = pieces_of(
        after(tokens, send_x), up_own, [((0, 0, 0, TOK, 0),), ((0, 1, 0, TOK, 0),)]
    )
    tok_core = swap_core(send_core)
    up_x = tok_x[:, PIECE:]
    up_pair = swap_core(jnp.concatenate([up_own, up_x]))
    block_2a = shift_y(block_1[:HALF], -1)
    block_2b = shift_y(block_3[HALF:], 1)
    blocks = (weight_bf, block_1, block_3, block_2a, block_2b)

    total = replica_step(after(pseudo_grad[0].astype(jnp.bfloat16), tok_core, for_far), lambda i: i ^ 6)
    total = replica_step(total, lambda i: i ^ 1)
    up_ready, total = lax.optimization_barrier((up_own, total))
    toks = (tok_own, tok_x, tok_core, tok_far)
    g0, to_above, to_below, keep_above, keep_below = weight_grad(toks, (up_ready, up_x, up_pair))
    from_below, from_above = shift_y(to_above, 1), shift_y(to_below, -1)

    before = input_grad((up_ready, up_x, up_pair), blocks[:3], PLACES[:3])
    ig_own, ig_x, ig_core, ig_far = input_grad(
        (after(up_ready, g0), up_x, up_pair), blocks[3:], PLACES[3:], before
    )
    back_x = swap_x(ig_x)
    back_far = swap_core(ig_far)
    back_core = swap_core(ig_core)
    other_a = swap_x(split(back_far))

    val_own, val_x, val_pair = value_parts(toks, (after(weight_bf, g0), *blocks[1:]))
    val_back = swap_core(val_pair)
    other_b = swap_x(after(pack(back_far, val_back, val_x), other_a))
    total = replica_step(after(total, back_core), lambda i: i ^ 2)

    s1, s3 = relay(after(keep_above, back_x), keep_below, from_below, from_above)
    r1 = shift_y(s1, 1)
    r3 = shift_y(s3, -1)

    total = replica_step(after(total, s1), lambda i: i ^ 8)
    new_momentum, new_global = outer_update(momentum, global_frag, total / 16)

    block = assemble(
        None,
        (ig_own, back_core, back_x, other_a),
        ((0, 0, 0, TOK), (0, 1, 0, TOK), (1, 0, 0, TOK), (1, 1, 0, FIRST)),
    )
    new_weight, new_m, new_v = adam(
        frag_index, (g0, from_above, r1, from_below, r3), adam_m[0], adam_v[0], master, after(new_global, block)
    )
    block, values = assemble(
        block, (after(other_b, new_weight),), ((1, 1, FIRST, TOK - FIRST),), (val_own, val_back)
    )
    return (
        values[None],
        block[None],
        new_weight[None],
        new_m[None],
        new_v[None],
        new_global,
        new_momentum,
    )


def solution(mesh):
    in_specs = (
        P("replica", "fsdp", None),
        P("replica", "fsdp", None),
        P("replica", "fsdp", None),
        P("replica", "fsdp", None),
        P("replica", "fsdp", None),
        P("replica", "fsdp", None),
        P("fsdp", None),
        P("fsdp", None),
        P(),
    )
    out_specs = (
        P("replica", "fsdp", None),
        P("replica", "fsdp", None),
        P("replica", "fsdp", None),
        P("replica", "fsdp", None),
        P("replica", "fsdp", None),
        P("fsdp", None),
        P("fsdp", None),
    )
    return jax.shard_map(body, mesh=mesh, in_specs=in_specs, out_specs=out_specs, check_vma=False)
```
